512 devices in a mesh: dp: 32 (over z, core), shard: 16 (over x, y).
Axes of the slice: x: 4, y: 4, z: 16, core: 2. Of those that a mesh axis runs over, the one named last changes fastest.
Arguments:
- activations: bfloat16 [5120, 64, 640], P(('dp', 'shard')), may hold values from -40 to 40
- cotangent: bfloat16 [3584, 64, 640], P(('dp', 'shard')), may hold values from -24 to 24
- window_len: int32 [32, 16, 10], P(None, 'shard'), may hold values from 0 to 64, as said below
- move_dest: int32 [32, 16, 10], P(None, 'shard'), may hold values from 0 to 31, as said below
- move_slot: int32 [32, 16, 10], P(None, 'shard'), may hold values from -1 to 6, as said below
- w_qkv: bfloat16 [640, 1920], P('shard'), may hold values from -0.25 to 0.25
- b_qkv: bfloat16 [1920], P('shard'), may hold values from -3 to 3
- norm_gain: bfloat16 [640], P('shard'), may hold values from 0.25 to 1.75
- w_out: bfloat16 [640, 640], P(None, 'shard'), may hold values from -0.25 to 0.25
Outputs:
- balanced_out: bfloat16 [3584, 64, 640], P(('dp', 'shard'))
- grad_input: bfloat16 [5120, 64, 640], P(('dp', 'shard'))
- grad_w_out: float32 [640, 640], P(None, 'shard')
The draws below stay inside these ranges and needn't reach their ends.
Inputs may be any that keep to these rules, and one draw needn't show every extreme that they name: `window_len`: 0 marks an empty slot. Every device holds 1 to 10 windows, at least one of 64 patches. `move_dest`: A window stays on its device or moves to one of the next 3 dp indices, wrapping; empty slots name their own index. A device sends at most one window to each other device and receives at most one; after the moves no device holds more than 7 windows, and some device holds 7. `move_slot`: -1 for empty slots; the windows that one device holds after the moves have distinct slots.
All inputs are finite; a program needn't handle non-finite values.
Results may differ from the reference program's by a relative error of at most 0.012.
Values may be sent and summed in bfloat16 or wider, within the bound.
No kernel may reach another device: no remote copies, remote signals or barrier semaphores. Data moves between devices by JAX's collectives and lax.ppermute only.
A program may use at most 64 MiB of HBM per device.

```python
import jax
import jax.numpy as jnp
from jax import lax

D = 640
HEADS = 8
HEAD = 80
PATCHES = 64
MOVES = 3
SLOTS = 10
INNER = 640
BAL = 7
WINDOWS = 5120
BWIN = 3584
N_DP = 32
N_SHARD = 16


def plan(key):
    group = MOVES + 1
    runs = N_DP // group
    kept_slots = SLOTS - MOVES

    def column(column_key):
        k_phase, k_sent, k_live, k_order = jax.random.split(column_key, 4)
        phase = jax.random.randint(k_phase, (), 0, group)
        devices = jnp.arange(N_DP, dtype=jnp.int32)
        shifted = (devices - phase) % N_DP
        offset = shifted % group
        run_ids = shifted // group
        sent_run = jax.random.randint(k_sent, (runs,), 1, MOVES + 1)
        sent_run = sent_run.at[0].set(MOVES)
        sent = sent_run[run_ids]
        light_live = jax.random.randint(k_live, (N_DP,), 1, kept_slots)
        heavy = offset == 0
        live_count = jnp.where(heavy, kept_slots + sent, light_live)
        orders = jax.vmap(lambda one_key: jax.random.permutation(one_key, SLOTS))(jax.random.split(k_order, N_DP))
        position = jnp.argsort(orders, axis=1).astype(jnp.int32)
        live = position < live_count[:, None]
        moved = heavy[:, None] & (position >= kept_slots) & live
        distance = position - kept_slots + 1
        target = jnp.where(moved, (devices[:, None] + distance) % N_DP, devices[:, None])
        landing = jnp.where(moved, light_live[target], position)
        landing = jnp.where(live, landing, -1)
        first = position == 0
        return (live, target, landing, first)
    column_keys = jax.random.split(key, N_SHARD)
    pieces = jax.vmap(column)(column_keys)
    return tuple((jnp.transpose(piece, (1, 0, 2)) for piece in pieces))


def draw_window_len(key, part):
    live, target, landing, first = plan(key)
    key = jax.random.fold_in(key, 7)
    k_part, k_whole = jax.random.split(key)
    partial_len = jax.random.randint(k_part, live.shape, 1, PATCHES + 1)
    whole = jax.random.randint(k_whole, live.shape, 0, 2) == 1
    length = jnp.where(whole | first, PATCHES, partial_len)
    return jnp.where(live, length, 0).astype(jnp.int32)


def draw_move_dest(key, part):
    live, target, landing, first = plan(key)
    return target.astype(jnp.int32)


def draw_move_slot(key, part):
    live, target, landing, first = plan(key)
    return landing.astype(jnp.int32)


def draw_activations(key, part):
    key = jax.random.fold_in(key, 3)
    k_base, k_rows, k_cols, k_common = jax.random.split(key, 4)
    base = jax.random.normal(k_base, (WINDOWS, PATCHES, D), jnp.float32)
    rows = jnp.exp(jax.random.uniform(k_rows, (WINDOWS, PATCHES, 1), jnp.float32, -1.15, 1.15))
    cols = jnp.exp(jax.random.uniform(k_cols, (D,), jnp.float32, -1.15, 1.15))
    return jnp.clip(base * rows * cols, -40.0, 40.0).astype(jnp.bfloat16)


def with_spikes(values, rng, source, target, blocks, factor):
    def block_of(axis_at):
        return (jnp.arange(values.shape[axis_at]) // (values.shape[axis_at] // blocks)).reshape((-1,) + (1,) * (values.ndim - 1 - axis_at))

    first = jax.random.permutation(rng, blocks)[block_of(target)]
    other_side = (block_of(target) + blocks // 2) % blocks
    return jnp.where((block_of(source) == first) | (block_of(source) == other_side), factor * values, values)


def level_of(own_key, extent, cuts, smallest, largest):
    factor_of = 1.0
    for dim, shards_of in cuts:
        heights = jax.random.uniform(jax.random.fold_in(jax.random.fold_in(own_key, 6), dim), (shards_of,), jnp.float32, smallest / len(cuts), largest / len(cuts))
        factor_of = factor_of * jnp.repeat(jnp.exp(heights), extent[dim] // shards_of).reshape((-1,) + (1,) * (len(extent) - 1 - dim))
    return factor_of


def noise(key, dims, scale, most, cuts=(), kind=jnp.bfloat16):
    drawn = jax.random.normal(key, dims, jnp.float32) * scale
    if len(cuts) > 0:
        drawn = level_of(key, dims, cuts, -0.22, 0.18) * drawn
    return jnp.clip(drawn, min=-most, max=most).astype(kind)


def gaussian_with(stream_key, shape, deviation, bound, shards, heavy, kind=jnp.bfloat16):
    drawn = deviation * jax.random.normal(stream_key, shape, jnp.float32)
    if shards:
        drawn = drawn * level_of(stream_key, shape, shards, -0.22, 0.18)
    return jnp.clip(with_spikes(drawn, jax.random.fold_in(stream_key, 3), *heavy), -bound, bound).astype(kind)


def setup_inputs(seed: int = 0) -> dict:
    streams_of = jax.random.split(jax.random.key(seed), 10)
    activations = draw_activations(jax.random.fold_in(streams_of[9], 71), 0)
    cotangent = gaussian_with(streams_of[1], (BWIN, PATCHES, D), 1.0, 24.0, ((0, 512),), (0, 2, 128, 5.5))
    window_len = draw_window_len(jax.random.fold_in(streams_of[9], 71), 0)
    move_dest = draw_move_dest(jax.random.fold_in(streams_of[9], 71), 0)
    move_slot = draw_move_slot(jax.random.fold_in(streams_of[9], 71), 0)
    w_qkv = noise(streams_of[5], (D, 3 * INNER), D ** -0.5, 0.25, ((0, 16),))
    b_qkv = noise(streams_of[6], (3 * INNER,), 0.5, 3.0, ((0, 16),))
    norm_gain = jnp.clip(1.0 + 0.15 * jax.random.normal(streams_of[7], (D,), jnp.float32), 0.25, 1.75).astype(jnp.bfloat16)
    w_out = noise(streams_of[8], (INNER, D), INNER ** -0.5, 0.25, ((1, 16),))
    return dict(activations=activations, cotangent=cotangent, window_len=window_len, move_dest=move_dest, move_slot=move_slot, w_qkv=w_qkv, b_qkv=b_qkv, norm_gain=norm_gain, w_out=w_out)


norm_eps = 1e-06

def window_block(windows_in, lengths, w_qkv, b_qkv, norm_gain, w_out):
    num_windows = windows_in.shape[0]
    head_shape = (num_windows, PATCHES, HEADS, HEAD)
    values = windows_in.astype(jnp.float32)
    inv_rms = lax.rsqrt(lax.optimization_barrier(jnp.mean(values * values, axis=-1, keepdims=True)) + norm_eps)
    normed = (values * inv_rms * norm_gain.astype(jnp.float32)).astype(jnp.bfloat16)
    projected = jnp.einsum('wpd,de->wpe', normed.astype(jnp.float32), w_qkv.astype(jnp.float32))
    projected = (projected + b_qkv.astype(jnp.float32)).astype(jnp.bfloat16)
    query_vecs = projected[..., :INNER].reshape(head_shape)
    key_vecs = projected[..., INNER:2 * INNER].reshape(head_shape)
    value_vecs = projected[..., 2 * INNER:].reshape(head_shape)
    scores = jnp.einsum('wqhe,wkhe->whqk', query_vecs.astype(jnp.float32), key_vecs.astype(jnp.float32)) * HEAD ** (-0.5)
    position = jnp.arange(PATCHES)
    allowed = position[None, :] < jnp.maximum(lengths, 1)[:, None]
    weights = jnp.where(allowed[:, None, None, :], jnp.exp(scores), 0.0)
    attn_probs = (weights / lax.optimization_barrier(jnp.sum(weights, axis=-1, keepdims=True))).astype(jnp.bfloat16)
    attended = jnp.einsum('whqk,wkhe->wqhe', attn_probs.astype(jnp.float32), value_vecs.astype(jnp.float32))
    attended = attended.astype(jnp.bfloat16).reshape(num_windows, PATCHES, INNER)
    projected_out = jnp.einsum('wpi,id->wpd', attended.astype(jnp.float32), w_out.astype(jnp.float32))
    row_mask = (position[None, :] < lengths[:, None]).astype(jnp.float32)[..., None]
    return (((values + projected_out) * row_mask).astype(jnp.bfloat16), attended)

def reference(activations, cotangent, window_len, move_dest, move_slot, w_qkv, b_qkv, norm_gain, w_out):
    shard_ids = jnp.arange(N_SHARD).astype(jnp.int32)[None, :, None]
    target = (move_dest * N_SHARD + shard_ids) * BAL + move_slot
    target = jnp.where(window_len > 0, target, BWIN).reshape(-1).astype(jnp.int32)
    upstream = jnp.take(cotangent, target, axis=0, mode='fill', fill_value=0)
    groups = N_DP * N_SHARD
    shape_blocks = (groups, SLOTS, PATCHES, D)
    blocks = (activations.reshape(shape_blocks), window_len.reshape(groups, SLOTS), upstream.reshape(shape_blocks))

    def one_group(running, group_item):
        windows_in, lengths, upstream_block = group_item
        result, backward, attended = jax.vjp(lambda inputs: window_block(inputs, lengths, w_qkv, b_qkv, norm_gain, w_out), windows_in, has_aux=True)
        grad_block, = backward(upstream_block)
        row_mask = (jnp.arange(PATCHES)[None, :] < lengths[:, None]).astype(jnp.bfloat16)[..., None]
        grad_term = jnp.einsum('wpi,wpd->id', attended.astype(jnp.float32), (upstream_block * row_mask).astype(jnp.float32))
        return (running + grad_term, (result, grad_block))
    grad_w_out, (results, grad_blocks) = lax.scan(one_group, jnp.zeros((INNER, D), jnp.float32), blocks)
    balanced_out = jnp.zeros((BWIN, PATCHES, D), jnp.bfloat16).at[target].set(results.reshape(WINDOWS, PATCHES, D), mode='drop')
    return (balanced_out, grad_blocks.reshape(WINDOWS, PATCHES, D), grad_w_out)
```

```python
import functools

import jax
import jax.numpy as jnp
from jax import lax
from jax.experimental import pallas as pl
from jax.experimental.pallas import tpu as pltpu
from jax.sharding import PartitionSpec as P

HEADS = 8
MOVES = 3
EPS = 1e-06
HALF = 320
PADH = 384
GROUP = 128
VMEM_LIMIT = 56 * 1024 * 1024

f32 = jnp.float32
bf16 = jnp.bfloat16


def permute_dp(array, by):
    n = lax.axis_size("dp")
    return lax.ppermute(array, "dp", [(i, (i + by) % n) for i in range(n)])


def swap_cores(array):
    n = lax.axis_size("dp")
    return lax.ppermute(array, "dp", [(i, i ^ 1) for i in range(n)])


def dot(a, b, ca, cb):
    return lax.dot_general(a, b, (((ca,), (cb,)), ((), ())), preferred_element_type=f32)


def pack_kernel(
    len_ref, dest_ref, slot_ref, act_ref, wqkv_ref, bias_ref, gain_ref, wout_ref,
    blob_ref, par_a_ref, par_b_ref, stage, pick, sems, blob_sems,
):
    n_dp = len_ref.shape[0]
    slots = len_ref.shape[2]
    n_shard = blob_ref.shape[0]
    me = lax.axis_index("dp")
    core = lax.rem(me, 2)
    for d in range(1, MOVES + 1):
        pick[d - 1] = 0
        target = lax.rem(me + d, n_dp)
        for s in range(slots):
            @pl.when((len_ref[me, 0, s] > 0) & (dest_ref[me, 0, s] == target))
            def _(d=d, s=s):
                pick[d - 1] = s
    moves = [
        pltpu.make_async_copy(act_ref.at[pick[1]], par_a_ref.at[0], sems.at[0]),
        pltpu.make_async_copy(act_ref.at[pick[2]], par_a_ref.at[1], sems.at[1]),
        pltpu.make_async_copy(act_ref.at[pick[0]], par_b_ref, sems.at[2]),
    ]
    for m in moves:
        m.start()
    inner = wout_ref.shape[0]
    wout_t = wout_ref[...].astype(f32).T.astype(bf16)
    stage[:, 4 * HALF:] = jnp.zeros((stage.shape[0], stage.shape[1] - 4 * HALF), bf16)
    for c in range(2):
        @pl.when(core == c)
        def _(c=c):
            stage[:, 0 : 4 * HALF] = jnp.concatenate(
                [
                    wqkv_ref[:, g * inner + c * HALF : g * inner + (c + 1) * HALF].astype(f32)
                    for g in range(3)
                ]
                + [wout_t[:, c * HALF : (c + 1) * HALF].astype(f32)],
                axis=1,
            ).astype(bf16)
    tail = jnp.concatenate(
        [
            jnp.pad(bias_ref[...].astype(f32), ((0, 0), (0, 128 - bias_ref.shape[1]))),
            jnp.pad(gain_ref[...].astype(f32), ((0, 0), (0, 128 - gain_ref.shape[1]))),
            jnp.zeros((14, 128), f32),
        ],
        axis=0,
    ).astype(bf16)
    stage[0:16, 4 * HALF :] = tail
    copies = [
        pltpu.make_async_copy(stage, blob_ref.at[s], blob_sems.at[s]) for s in range(n_shard)
    ]
    for cp in copies:
        cp.start()
    for cp in copies:
        cp.wait()
    for m in moves:
        m.wait()


def pack(tables, act, wqkv, bias, gain, wout, n_shard):
    rows = wqkv.shape[0]
    cols = 4 * HALF + 128
    window = act.shape[1:]
    smem = pl.BlockSpec(memory_space=pltpu.SMEM)
    vmem = pl.BlockSpec(memory_space=pltpu.VMEM)
    hbm = pl.BlockSpec(memory_space=pl.ANY)
    return pl.pallas_call(
        pack_kernel,
        out_shape=(
            jax.ShapeDtypeStruct((n_shard, rows, cols), bf16),
            jax.ShapeDtypeStruct((2,) + window, bf16),
            jax.ShapeDtypeStruct(window, bf16),
        ),
        in_specs=[smem, smem, smem, hbm, vmem, vmem, vmem, vmem],
        out_specs=(hbm, hbm, hbm),
        scratch_shapes=[
            pltpu.VMEM((rows, cols), bf16),
            pltpu.SMEM((MOVES,), jnp.int32),
            pltpu.SemaphoreType.DMA((MOVES,)),
            pltpu.SemaphoreType.DMA((n_shard,)),
        ],
        compiler_params=pltpu.CompilerParams(vmem_limit_bytes=VMEM_LIMIT),
        name="pack_weights",
    )(*tables, act, wqkv, bias, gain, wout)


def block_kernel(
    len_ref, dest_ref, slot_ref, act_ref, arr_a_ref, arr_b_ref, cot_ref, own_ref, oth_ref,
    out_ref, grad_ref, ret_c_ref, ret_d_ref, gt_own_ref, gt_oth_ref,
    xb, cotb, g_own, g_oth, gbuf, zeros, bias_row, gain_row, nrm, ub, wqkv, wo, qkv, da, att, dproj,
    code, lens, win_sems, load_sems, out_sems,
):
    n_dp = len_ref.shape[0]
    slots = len_ref.shape[2]
    kept = xb.shape[0]
    patches, ch = xb.shape[1:]
    n_shard, rows = own_ref.shape[:2]
    tokens = kept * patches
    me = lax.axis_index("dp")
    core = lax.rem(me, 2)

    loads = [
        pltpu.make_async_copy(own_ref, g_own, load_sems.at[0]),
        pltpu.make_async_copy(oth_ref, g_oth, load_sems.at[1]),
        pltpu.make_async_copy(cot_ref, cotb, load_sems.at[2]),
    ]
    for cp in loads:
        cp.start()
    xb[...] = jnp.zeros(xb.shape, bf16)
    zeros[...] = jnp.zeros(zeros.shape, bf16)
    for b in range(kept):
        code[b] = -1
        lens[b] = 0
    arrived = {1: arr_b_ref.at[0], 2: arr_a_ref.at[0], 3: arr_b_ref.at[1]}
    for d in range(MOVES + 1):
        row = lax.rem(me - d + n_dp, n_dp)
        for s in range(slots):
            @pl.when((len_ref[row, 0, s] > 0) & (dest_ref[row, 0, s] == me))
            def _(d=d, s=s, row=row):
                b = slot_ref[row, 0, s]
                code[b] = d
                lens[b] = len_ref[row, 0, s]
                source = act_ref.at[s] if d == 0 else arrived[d]
                pltpu.make_async_copy(source, xb.at[b], win_sems.at[b]).start()

    loads[0].wait()
    for s in range(n_shard):
        tail = g_own[s, 0:16, 4 * HALF :].astype(f32)
        bias_row[0:1, 120 * s : 120 * s + 120] = tail[0:1, 0:120]
        gain_row[0:1, rows * s : rows * s + rows] = tail[1:2, 0:rows]
    loads[1].wait()
    pad = jnp.zeros((2 * rows, PADH - HALF), f32)
    for h, g in enumerate((g_own, g_oth)):
        for t in range(n_shard // 2):
            both = jnp.concatenate(
                [g[2 * t, :, 0 : 4 * HALF].astype(f32), g[2 * t + 1, :, 0 : 4 * HALF].astype(f32)],
                axis=0,
            )
            at = pl.ds(2 * rows * t, 2 * rows)
            for k in range(4):
                piece = jnp.concatenate(
                    [both[:, k * HALF : (k + 1) * HALF], pad], axis=1
                ).astype(bf16)
                if k < 3:
                    wqkv[at, (3 * h + k) * PADH : (3 * h + k + 1) * PADH] = piece
                else:
                    wo[at, h * PADH : (h + 1) * PADH] = piece

    bias = []
    for h in range(2):
        for k in range(3):
            low = bias_row[0:1, 2 * k * HALF : (2 * k + 1) * HALF]
            high = bias_row[0:1, (2 * k + 1) * HALF : (2 * k + 2) * HALF]
            first = core == h
            bias.append(jnp.where(first, low, high))
            bias.append(jnp.zeros((1, PADH - HALF), f32))
    bias = jnp.concatenate(bias, axis=1)

    loads[2].wait()
    position = lax.broadcasted_iota(jnp.int32, (patches, 1), 0)
    gain = gain_row[...]
    for b in range(kept):
        @pl.when(code[b] >= 0)
        def _(b=b):
            pltpu.make_async_copy(act_ref.at[0], xb.at[b], win_sems.at[b]).wait()

        x = xb[b].astype(f32)
        inv = lax.rsqrt(jnp.mean(x * x, axis=-1, keepdims=True) + EPS)
        at = pl.ds(b * patches, patches)
        nrm[at, :] = (x * inv * gain).astype(bf16)
        live = position < lens[b]
        ub[at, :] = jnp.where(live, cotb[b].astype(f32), 0.0).astype(bf16)

    qkv[0:tokens, :] = (dot(nrm[...], wqkv[...], 1, 0) + bias).astype(bf16)
    qkv[tokens:, :] = jnp.zeros((qkv.shape[0] - tokens, qkv.shape[1]), bf16)
    da[0:tokens, :] = dot(ub[...], wo[...], 1, 0).astype(bf16)
    da[tokens:, :] = jnp.zeros((da.shape[0] - tokens, da.shape[1]), bf16)

    heads = 4
    head = HALF // heads
    scale = head ** (-0.5)
    lane_head = lax.broadcasted_iota(jnp.int32, (GROUP, PADH), 1) // head
    head_mask = [(lane_head == h).astype(f32).astype(bf16) for h in range(heads)]
    q_pos = lax.broadcasted_iota(jnp.int32, (GROUP, GROUP), 0)
    k_pos = lax.broadcasted_iota(jnp.int32, (GROUP, GROUP), 1)
    lower = jnp.where(q_pos < patches, 0, patches)

    def by_head(m):
        return jnp.concatenate([m * head_mask[h] for h in range(heads)], axis=0)

    def pair(j, _):
        at = pl.ds(pl.multiple_of(j * GROUP, GROUP), GROUP)
        len0 = jnp.maximum(lens[2 * j], 1)
        second = jnp.minimum(2 * j + 1, kept - 1)
        len1 = jnp.maximum(lens[second], 1)
        upper = jnp.where(q_pos < patches, len0, patches + len1)
        allowed = (k_pos >= lower) & (k_pos < upper)
        for h in range(2):
            base = 3 * h * PADH
            q = qkv[at, base : base + PADH]
            k = qkv[at, base + PADH : base + 2 * PADH]
            v = qkv[at, base + 2 * PADH : base + 3 * PADH]
            d_att = da[at, h * PADH : (h + 1) * PADH]
            k_heads = by_head(k)
            v_heads = by_head(v)
            scores = dot(q, k_heads, 1, 1) * scale
            d_probs = dot(d_att, v_heads, 1, 1)
            probs, d_scores = [], []
            for i in range(heads):
                lanes = slice(i * GROUP, (i + 1) * GROUP)
                weights = jnp.where(allowed, jnp.exp(scores[:, lanes]), 0.0)
                p = weights / jnp.sum(weights, axis=-1, keepdims=True)
                dp = d_probs[:, lanes].astype(bf16).astype(f32)
                mean = jnp.sum(dp * p, axis=-1, keepdims=True)
                probs.append(p.astype(bf16))
                d_scores.append((p * (dp - mean) * scale).astype(bf16))
            att[at, h * PADH : (h + 1) * PADH] = dot(
                jnp.concatenate(probs, axis=1), v_heads, 1, 0
            ).astype(bf16)
            dproj[at, base : base + PADH] = dot(
                jnp.concatenate(d_scores, axis=1), k_heads, 1, 0
            ).astype(bf16)
            dproj[at, base + PADH : base + 2 * PADH] = dot(
                jnp.concatenate(d_scores, axis=0), by_head(q), 0, 0
            ).astype(bf16)
            dproj[at, base + 2 * PADH : base + 3 * PADH] = dot(
                jnp.concatenate(probs, axis=0), by_head(d_att), 0, 0
            ).astype(bf16)
        return 0

    lax.fori_loop(0, qkv.shape[0] // GROUP, pair, 0)

    attended = att[0:tokens, :]
    gt = dot(ub[...], attended, 0, 0)
    gt_own_ref[...] = gt[:, 0:HALF]
    gt_oth_ref[...] = gt[:, PADH : PADH + HALF].astype(bf16)
    added = dot(attended, wo[...], 1, 1)
    d_nrm = dot(dproj[0:tokens, :], wqkv[...], 1, 1)
    for b in range(kept):
        at = slice(b * patches, (b + 1) * patches)
        x = xb[b].astype(f32)
        live = position < lens[b]
        out_ref[b] = jnp.where(live, x + added[at], 0.0).astype(bf16)
        inv = lax.rsqrt(jnp.mean(x * x, axis=-1, keepdims=True) + EPS)
        t = d_nrm[at].astype(bf16).astype(f32) * gain
        along = jnp.mean(t * x, axis=-1, keepdims=True)
        dx = t * inv - x * (inv * inv * inv * along)
        gbuf[b] = (ub[at, :].astype(f32) + dx).astype(bf16)

    def own_copy(s, source):
        return pltpu.make_async_copy(source, grad_ref.at[s], out_sems.at[s])

    for s in range(slots):
        stays = (len_ref[me, 0, s] > 0) & (dest_ref[me, 0, s] == me)

        @pl.when(stays)
        def _(s=s):
            own_copy(s, gbuf.at[slot_ref[me, 0, s]]).start()

        @pl.when(jnp.logical_not(stays))
        def _(s=s):
            own_copy(s, zeros).start()

    returned = {1: ret_c_ref.at[0], 2: ret_d_ref, 3: ret_c_ref.at[1]}
    for b in range(kept):
        for d in range(1, MOVES + 1):
            @pl.when(code[b] == d)
            def _(b=b, d=d):
                cp = pltpu.make_async_copy(gbuf.at[b], returned[d], win_sems.at[b])
                cp.start()
                cp.wait()
    for s in range(slots):
        own_copy(s, zeros).wait()


def block(tables, act, arr_a, arr_b, cot, own, oth):
    kept, patches, ch = cot.shape
    slots = act.shape[0]
    tokens = kept * patches
    padded = -(-tokens // GROUP) * GROUP
    smem = pl.BlockSpec(memory_space=pltpu.SMEM)
    vmem = pl.BlockSpec(memory_space=pltpu.VMEM)
    hbm = pl.BlockSpec(memory_space=pl.ANY)
    window = (patches, ch)
    return pl.pallas_call(
        block_kernel,
        out_shape=(
            jax.ShapeDtypeStruct(cot.shape, bf16),
            jax.ShapeDtypeStruct(act.shape, bf16),
            jax.ShapeDtypeStruct((2,) + window, bf16),
            jax.ShapeDtypeStruct(window, bf16),
            jax.ShapeDtypeStruct((ch, HALF), f32),
            jax.ShapeDtypeStruct((ch, HALF), bf16),
        ),
        in_specs=[smem] * 3 + [hbm] * 6,
        out_specs=(vmem, hbm, hbm, hbm, vmem, vmem),
        scratch_shapes=[
            pltpu.VMEM(cot.shape, bf16),
            pltpu.VMEM(cot.shape, bf16),
            pltpu.VMEM(own.shape, bf16),
            pltpu.VMEM(own.shape, bf16),
            pltpu.VMEM(cot.shape, bf16),
            pltpu.VMEM(window, bf16),
            pltpu.VMEM((1, 6 * HALF), f32),
            pltpu.VMEM((1, ch), f32),
            pltpu.VMEM((tokens, ch), bf16),
            pltpu.VMEM((tokens, ch), bf16),
            pltpu.VMEM((ch, 6 * PADH), bf16),
            pltpu.VMEM((ch, 2 * PADH), bf16),
            pltpu.VMEM((padded, 6 * PADH), bf16),
            pltpu.VMEM((padded, 2 * PADH), bf16),
            pltpu.VMEM((padded, 2 * PADH), bf16),
            pltpu.VMEM((padded, 6 * PADH), bf16),
            pltpu.SMEM((kept,), jnp.int32),
            pltpu.SMEM((kept,), jnp.int32),
            pltpu.SemaphoreType.DMA((kept,)),
            pltpu.SemaphoreType.DMA((3,)),
            pltpu.SemaphoreType.DMA((slots,)),
        ],
        compiler_params=pltpu.CompilerParams(vmem_limit_bytes=VMEM_LIMIT),
        name="window_block",
    )(*tables, act, arr_a, arr_b, cot, own, oth)


def place_kernel(len_ref, dest_ref, back_c_ref, back_d_ref, grad_in_ref, grad_ref, sems):
    n_dp = len_ref.shape[0]
    slots = len_ref.shape[2]
    me = lax.axis_index("dp")
    back = {1: back_c_ref.at[0], 2: back_d_ref.at[0], 3: back_d_ref.at[1]}
    for wait in (False, True):
        for d in range(1, MOVES + 1):
            target = lax.rem(me + d, n_dp)
            for s in range(slots):
                @pl.when((len_ref[me, 0, s] > 0) & (dest_ref[me, 0, s] == target))
                def _(d=d, s=s, wait=wait):
                    cp = pltpu.make_async_copy(back[d], grad_ref.at[s], sems.at[d - 1])
                    if wait:
                        cp.wait()
                    else:
                        cp.start()


def place(tables, back_c, back_d, grad):
    smem = pl.BlockSpec(memory_space=pltpu.SMEM)
    hbm = pl.BlockSpec(memory_space=pl.ANY)
    return pl.pallas_call(
        place_kernel,
        out_shape=jax.ShapeDtypeStruct(grad.shape, bf16),
        in_specs=[smem, smem, hbm, hbm, hbm],
        out_specs=hbm,
        scratch_shapes=[pltpu.SemaphoreType.DMA((MOVES,))],
        input_output_aliases={4: 0},
        name="place_returned",
    )(tables[0], tables[1], back_c, back_d, grad)


def add_kernel(parts_ref, out_ref):
    n = parts_ref.shape[0]
    for c in range(2):
        total = parts_ref[c].astype(f32)
        for z in range(1, n // 2):
            total = total + parts_ref[2 * z + c].astype(f32)
        out_ref[c * HALF : (c + 1) * HALF, :] = total.T


def add_shares(parts):
    n, rows, half = parts.shape
    vmem = pl.BlockSpec(memory_space=pltpu.VMEM)
    return pl.pallas_call(
        add_kernel,
        out_shape=jax.ShapeDtypeStruct((2 * half, rows), f32),
        in_specs=[vmem],
        out_specs=vmem,
        compiler_params=pltpu.CompilerParams(vmem_limit_bytes=VMEM_LIMIT),
        name="add_shares",
    )(parts)


def shards(
    activations, cotangent, window_len, move_dest, move_slot, w_qkv, b_qkv, norm_gain, w_out
):
    n_shard = lax.axis_size("shard")
    rows = w_qkv.shape[0]
    tables = (window_len, move_dest, move_slot)
    blob, par_a, par_b = pack(
        tables, activations, w_qkv, b_qkv[None], norm_gain[None], w_out, n_shard
    )
    arr_a = permute_dp(par_a, 2)
    own = lax.all_to_all(blob, "shard", 0, 0)
    arr_b = permute_dp(jnp.stack([par_b, arr_a[1]]), 1)
    oth = swap_cores(own)
    out, grad, ret_c, ret_d, gt_own, gt_oth = block(
        tables, activations, arr_a, arr_b, cotangent, own, oth
    )
    gt_in = swap_cores(gt_oth)
    back_c = permute_dp(ret_c, -1)
    share = (gt_own + gt_in.astype(f32)).astype(bf16).reshape(n_shard, rows, HALF)
    chunks = lax.all_to_all(share, "shard", 0, 0)
    summed = jnp.sum(chunks.astype(f32), axis=0).astype(bf16)
    back_d = permute_dp(jnp.stack([ret_d, back_c[1]]), -2)
    parts = lax.all_gather(summed, "dp", axis=0)
    grad_w_out = add_shares(parts)
    grad_input = place(tables, back_c, back_d, grad)
    return (out, grad_input, grad_w_out)


def solution(mesh):
    return jax.shard_map(
        shards,
        mesh=mesh,
        in_specs=(
            P(("dp", "shard"), None, None),
            P(("dp", "shard"), None, None),
            P(None, "shard", None),
            P(None, "shard", None),
            P(None, "shard", None),
            P("shard", None),
            P("shard"),
            P("shard"),
            P(None, "shard"),
        ),
        out_specs=(
            P(("dp", "shard"), None, None),
            P(("dp", "shard"), None, None),
            P(None, "shard"),
        ),
        check_vma=False,
    )
```

```python
import functools

import jax
import jax.numpy as jnp
from jax import lax
from jax.experimental import pallas as pl
from jax.experimental.pallas import tpu as pltpu
from jax.sharding import PartitionSpec as P

HEADS = 8
MOVES = 3
EPS = 1e-06
HALF = 320
PADH = 384
CODES, LENS, STAYS, LEAVES, PLAN = 0, 16, 32, 48, 64
VMEM_LIMIT = 40 * 1024 * 1024
PACK_VMEM_LIMIT = 60 * 1024 * 1024

f32 = jnp.float32
bf16 = jnp.bfloat16


def permute_dp(array, by):
    n = lax.axis_size("dp")
    return lax.ppermute(array, "dp", [(i, (i + by) % n) for i in range(n)])


def swap_cores(array):
    n = lax.axis_size("dp")
    return lax.ppermute(array, "dp", [(i, i ^ 1) for i in range(n)])


def dot(a, b, ca, cb):
    return lax.dot_general(a, b, (((ca,), (cb,)), ((), ())), preferred_element_type=f32)


def pack_kernel(
    len_ref, dest_ref, slot_ref, act_ref, wqkv_ref, bias_ref, gain_ref, wout_ref,
    blob_ref, par_a_ref, par_b_ref, plan_ref, stage, sems, blob_sems,
):
    slots, _, n_dp = len_ref.shape
    n_shard = blob_ref.shape[0]
    inner = wout_ref.shape[1]
    me = lax.axis_index("dp")
    core = lax.rem(me, 2)
    for i in range(plan_ref.shape[0]):
        plan_ref[i] = 0 if LENS <= i < STAYS else -1
    for s in range(slots):
        live = len_ref[s, 0, me] > 0
        dest = dest_ref[s, 0, me]

        @pl.when(live & (dest == me))
        def _(s=s):
            b = slot_ref[s, 0, me]
            plan_ref[CODES + b] = s
            plan_ref[LENS + b] = len_ref[s, 0, me]
            plan_ref[STAYS + s] = b

        for d in range(1, MOVES + 1):
            @pl.when(live & (dest == lax.rem(me + d, n_dp)))
            def _(d=d, s=s):
                plan_ref[LEAVES + d] = s

    leaving = [
        pltpu.make_async_copy(
            act_ref.at[jnp.maximum(plan_ref[LEAVES + d], 0)], to, sems.at[d - 1]
        )
        for d, to in ((1, par_b_ref), (2, par_a_ref.at[0]), (3, par_a_ref.at[1]))
    ]
    for cp in leaving:
        cp.start()

    for c in range(2):
        @pl.when(core == c)
        def _(c=c):
            stage[:, 0 : 4 * HALF] = jnp.concatenate(
                [
                    wqkv_ref[:, g * inner + c * HALF : g * inner + (c + 1) * HALF].astype(f32)
                    for g in range(3)
                ]
                + [wout_ref[:, c * HALF : (c + 1) * HALF].astype(f32)],
                axis=1,
            ).astype(bf16)
    stage[:, 4 * HALF :] = jnp.zeros((stage.shape[0], stage.shape[1] - 4 * HALF), bf16)
    tail = jnp.concatenate(
        [
            jnp.pad(bias_ref[...].astype(f32), ((0, 0), (0, 128 - bias_ref.shape[1]))),
            jnp.pad(gain_ref[...].astype(f32), ((0, 0), (0, 128 - gain_ref.shape[1]))),
            jnp.zeros((14, 128), f32),
        ],
        axis=0,
    ).astype(bf16)
    stage[0:16, 4 * HALF :] = tail
    copies = [
        pltpu.make_async_copy(stage, blob_ref.at[s], blob_sems.at[s]) for s in range(n_shard)
    ]
    for cp in copies:
        cp.start()

    for d in range(1, MOVES + 1):
        row = lax.rem(me - d + n_dp, n_dp)
        for s in range(slots):
            @pl.when((len_ref[s, 0, row] > 0) & (dest_ref[s, 0, row] == me))
            def _(d=d, s=s, row=row):
                b = slot_ref[s, 0, row]
                plan_ref[CODES + b] = slots + d - 1
                plan_ref[LENS + b] = len_ref[s, 0, row]

    for cp in leaving:
        cp.wait()
    for cp in copies:
        cp.wait()


def pack(tables, act, wqkv, bias, gain, wout_t, n_shard):
    rows = wqkv.shape[0]
    cols = 4 * HALF + 128
    window = act.shape[1:]
    smem = pl.BlockSpec(memory_space=pltpu.SMEM)
    vmem = pl.BlockSpec(memory_space=pltpu.VMEM)
    hbm = pl.BlockSpec(memory_space=pl.ANY)
    return pl.pallas_call(
        pack_kernel,
        out_shape=(
            jax.ShapeDtypeStruct((n_shard, rows, cols), bf16),
            jax.ShapeDtypeStruct((2,) + window, bf16),
            jax.ShapeDtypeStruct(window, bf16),
            jax.ShapeDtypeStruct((PLAN,), jnp.int32),
        ),
        in_specs=[smem, smem, smem, hbm, vmem, vmem, vmem, vmem],
        out_specs=(hbm, vmem, vmem, smem),
        scratch_shapes=[
            pltpu.VMEM((rows, cols), bf16),
            pltpu.SemaphoreType.DMA((MOVES,)),
            pltpu.SemaphoreType.DMA((n_shard,)),
        ],
        compiler_params=pltpu.CompilerParams(vmem_limit_bytes=PACK_VMEM_LIMIT),
        name="pack_weights",
    )(*tables, act, wqkv, bias, gain, wout_t)


def block_kernel(
    plan_ref, act_ref, arr_a_ref, arr_b_ref, cot_ref, g_own, g_oth,
    out_ref, grad_ref, ret_c_ref, ret_d_ref, gt_own_ref, gt_oth_ref,
    xb, cotb, gbuf, zeros, bias_row, gain_row, nrm, ub, wqkv, wo, qkv, da, att, dproj, gt_own, gt_oth,
    win_sems, load_sems, out_sems,
):
    slots = act_ref.shape[0]
    kept = xb.shape[0]
    patches, ch = xb.shape[1:]
    n_shard, rows = g_own.shape[:2]
    tokens = kept * patches
    me = lax.axis_index("dp")
    core = lax.rem(me, 2)

    loads = [
        pltpu.make_async_copy(cot_ref, cotb, load_sems.at[0]),
    ]
    for cp in loads:
        cp.start()
    xb[...] = jnp.zeros(xb.shape, bf16)
    zeros[...] = jnp.zeros(zeros.shape, bf16)
    code = [plan_ref[CODES + b] for b in range(kept)]
    lens = [plan_ref[LENS + b] for b in range(kept)]
    arrived = [arr_b_ref.at[0], arr_a_ref.at[0], arr_b_ref.at[1]]
    for b in range(kept):
        @pl.when((code[b] >= 0) & (code[b] < slots))
        def _(b=b):
            pltpu.make_async_copy(act_ref.at[code[b]], xb.at[b], win_sems.at[b]).start()

        for d in range(MOVES):
            @pl.when(code[b] == slots + d)
            def _(b=b, d=d):
                pltpu.make_async_copy(arrived[d], xb.at[b], win_sems.at[b]).start()

    def zero_copy(s):
        return pltpu.make_async_copy(zeros, grad_ref.at[s], out_sems.at[s])

    for s in range(slots):
        @pl.when(plan_ref[STAYS + s] < 0)
        def _(s=s):
            zero_copy(s).start()

    returned = [ret_c_ref.at[0], ret_d_ref, ret_c_ref.at[1]]

    def ready(b):
        @pl.when((code[b] >= 0) & (code[b] < slots))
        def _():
            pltpu.make_async_copy(gbuf.at[b], grad_ref.at[code[b]], win_sems.at[b]).start()

        for d in range(MOVES):
            @pl.when(code[b] == slots + d)
            def _(d=d):
                pltpu.make_async_copy(gbuf.at[b], returned[d], win_sems.at[b]).start()

    for s in range(n_shard):
        tail = g_own[s, 0:16, 4 * HALF :].astype(f32)
        bias_row[0:1, 120 * s : 120 * s + 120] = tail[0:1, 0:120]
        gain_row[0:1, rows * s : rows * s + rows] = tail[1:2, 0:rows]
    pad = jnp.zeros((2 * rows, PADH - HALF), f32)
    for h, g in enumerate((g_own, g_oth)):
        for t in range(n_shard // 2):
            both = jnp.concatenate(
                [g[2 * t, :, 0 : 4 * HALF].astype(f32), g[2 * t + 1, :, 0 : 4 * HALF].astype(f32)],
                axis=0,
            )
            at = pl.ds(2 * rows * t, 2 * rows)
            for k in range(4):
                piece = jnp.concatenate(
                    [both[:, k * HALF : (k + 1) * HALF], pad], axis=1
                ).astype(bf16)
                if k < 3:
                    wqkv[at, (3 * h + k) * PADH : (3 * h + k + 1) * PADH] = piece
                else:
                    wo[at, h * PADH : (h + 1) * PADH] = piece

    bias = []
    for h in range(2):
        for k in range(3):
            low = bias_row[0:1, 2 * k * HALF : (2 * k + 1) * HALF]
            high = bias_row[0:1, (2 * k + 1) * HALF : (2 * k + 2) * HALF]
            first = core == h
            bias.append(jnp.where(first, low, high))
            bias.append(jnp.zeros((1, PADH - HALF), f32))
    bias = jnp.concatenate(bias, axis=1)

    loads[0].wait()
    position = lax.broadcasted_iota(jnp.int32, (patches, 1), 0)
    gain = gain_row[...]
    for b in range(kept):
        @pl.when(code[b] >= 0)
        def _(b=b):
            pltpu.make_async_copy(act_ref.at[0], xb.at[b], win_sems.at[b]).wait()

        x = xb[b].astype(f32)
        inv = lax.rsqrt(jnp.mean(x * x, axis=-1, keepdims=True) + EPS)
        at = pl.ds(b * patches, patches)
        nrm[at, :] = (x * inv * gain).astype(bf16)
        live = position < lens[b]
        ub[at, :] = jnp.where(live, cotb[b].astype(f32), 0.0).astype(bf16)

    qkv[...] = (dot(nrm[...], wqkv[...], 1, 0) + bias).astype(bf16)
    da[...] = dot(ub[...], wo[...], 1, 0).astype(bf16)

    head = HALF // 4
    scale = head ** (-0.5)
    lanes = (slice(0, 256), slice(128, 384))
    lane = lax.broadcasted_iota(jnp.int32, (patches, 256), 1)
    masks = []
    for i in range(4):
        low = i * head - lanes[i // 2].start
        masks.append(((lane >= low) & (lane < low + head)).astype(f32))
    low_masks = [m.astype(bf16) for m in masks]
    key_pos = lax.broadcasted_iota(jnp.int32, (patches, 2 * patches), 0)

    def by_head(m, g):
        return jnp.concatenate([m * low_masks[2 * g], m * low_masks[2 * g + 1]], axis=0)

    def joined(a, b):
        return jnp.concatenate([a[:, :128], a[:, 128:] + b[:, :128], b[:, 128:]], axis=1).astype(bf16)

    def stacked(m):
        return jnp.concatenate([m[:, :patches], m[:, patches:]], axis=0)

    def scored(w, h, g):
        at = pl.ds(w * patches, patches)
        base = 3 * h * PADH
        low = lanes[g].start
        q, k, v = [
            qkv[at, base + i * PADH + low : base + i * PADH + low + 256] for i in range(3)
        ]
        q_heads = by_head(q, g)
        d_heads = by_head(da[at, h * PADH + low : h * PADH + low + 256], g)
        return q_heads, d_heads, k, v, dot(k, q_heads, 1, 1), dot(v, d_heads, 1, 1)

    def softmaxed(w, h, g, q_heads, d_heads, k, v, scores, d_probs):
        allowed = key_pos < jnp.maximum(lens[w], 1)
        weights = jnp.where(allowed, jnp.exp(scores * scale), 0.0)
        probs = weights * (1.0 / jnp.sum(weights, axis=0, keepdims=True))
        d_probs = d_probs.astype(bf16).astype(f32)
        mean = jnp.sum(d_probs * probs, axis=0, keepdims=True)
        d_scores = (probs * (d_probs - mean) * scale).astype(bf16)
        return q_heads, d_heads, k, v, probs.astype(bf16), d_scores

    def combined(w, h, g, q_heads, d_heads, k, v, probs, d_scores):
        return (
            dot(stacked(probs), by_head(v, g), 0, 0),
            dot(stacked(d_scores), by_head(k, g), 0, 0),
            dot(d_scores, q_heads, 1, 0),
            dot(probs, d_heads, 1, 0),
        )

    def stored(w, h, first, second):
        at = pl.ds(w * patches, patches)
        base = 3 * h * PADH
        o, dq, dk, dv = [joined(x, y) for x, y in zip(first, second)]
        att[at, h * PADH : (h + 1) * PADH] = o
        dproj[at, base : base + PADH] = dq
        dproj[at, base + PADH : base + 2 * PADH] = dk
        dproj[at, base + 2 * PADH : base + 3 * PADH] = dv

    todo = [(w, h, g) for w in range(kept) for h in range(2) for g in range(2)]
    step = 14
    for first in range(0, len(todo), step):
        some = todo[first : first + step]
        state = [scored(*p) for p in some]
        state = [softmaxed(*p, *c) for p, c in zip(some, state)]
        state = [combined(*p, *c) for p, c in zip(some, state)]
        for i in range(0, len(some), 2):
            stored(some[i][0], some[i][1], state[i], state[i + 1])

    attended = att[...]
    gt = dot(ub[...], attended, 0, 0)
    gt_own[...] = gt[:, 0:HALF]
    gt_oth[...] = gt[:, PADH : PADH + HALF].astype(bf16)
    done = [
        pltpu.make_async_copy(gt_oth, gt_oth_ref, load_sems.at[0]),
        pltpu.make_async_copy(gt_own, gt_own_ref, load_sems.at[1]),
    ]
    for cp in done:
        cp.start()
    added = dot(attended, wo[...], 1, 1)
    for b in range(kept):
        at = slice(b * patches, (b + 1) * patches)
        live = position < lens[b]
        cotb[b] = jnp.where(live, xb[b].astype(f32) + added[at], 0.0).astype(bf16)
    done.append(pltpu.make_async_copy(cotb, out_ref, load_sems.at[2]))
    done[2].start()
    d_nrm = dot(dproj[...], wqkv[...], 1, 1)
    for b in range(kept):
        at = slice(b * patches, (b + 1) * patches)
        x = xb[b].astype(f32)
        inv = lax.rsqrt(jnp.mean(x * x, axis=-1, keepdims=True) + EPS)
        t = d_nrm[at].astype(bf16).astype(f32) * gain
        along = jnp.mean(t * x, axis=-1, keepdims=True)
        dx = t * inv - x * (inv * inv * inv * along)
        gbuf[b] = (ub[at, :].astype(f32) + dx).astype(bf16)
        ready(b)

    for b in range(kept):
        @pl.when(code[b] >= 0)
        def _(b=b):
            pltpu.make_async_copy(gbuf.at[b], grad_ref.at[0], win_sems.at[b]).wait()
    for s in range(slots):
        @pl.when(plan_ref[STAYS + s] < 0)
        def _(s=s):
            zero_copy(s).wait()
    for cp in done:
        cp.wait()


def block(plan, act, arr_a, arr_b, cot, own, oth):
    kept, patches, ch = cot.shape
    slots = act.shape[0]
    tokens = kept * patches
    smem = pl.BlockSpec(memory_space=pltpu.SMEM)
    vmem = pl.BlockSpec(memory_space=pltpu.VMEM)
    hbm = pl.BlockSpec(memory_space=pl.ANY)
    window = (patches, ch)
    return pl.pallas_call(
        block_kernel,
        out_shape=(
            jax.ShapeDtypeStruct(cot.shape, bf16),
            jax.ShapeDtypeStruct(act.shape, bf16),
            jax.ShapeDtypeStruct((2,) + window, bf16),
            jax.ShapeDtypeStruct(window, bf16),
            jax.ShapeDtypeStruct((ch, HALF), f32),
            jax.ShapeDtypeStruct((ch, HALF), bf16),
        ),
        in_specs=[smem] + [hbm] * 4 + [vmem] * 2,
        out_specs=(hbm,) * 6,
        scratch_shapes=[
            pltpu.VMEM(cot.shape, bf16),
            pltpu.VMEM(cot.shape, bf16),
            pltpu.VMEM(cot.shape, bf16),
            pltpu.VMEM(window, bf16),
            pltpu.VMEM((1, 6 * HALF), f32),
            pltpu.VMEM((1, ch), f32),
            pltpu.VMEM((tokens, ch), bf16),
            pltpu.VMEM((tokens, ch), bf16),
            pltpu.VMEM((ch, 6 * PADH), bf16),
            pltpu.VMEM((ch, 2 * PADH), bf16),
            pltpu.VMEM((tokens, 6 * PADH), bf16),
            pltpu.VMEM((tokens, 2 * PADH), bf16),
            pltpu.VMEM((tokens, 2 * PADH), bf16),
            pltpu.VMEM((tokens, 6 * PADH), bf16),
            pltpu.VMEM((ch, HALF), f32),
            pltpu.VMEM((ch, HALF), bf16),
            pltpu.SemaphoreType.DMA((kept,)),
            pltpu.SemaphoreType.DMA((3,)),
            pltpu.SemaphoreType.DMA((slots,)),
        ],
        compiler_params=pltpu.CompilerParams(vmem_limit_bytes=VMEM_LIMIT),
        name="window_block",
    )(plan, act, arr_a, arr_b, cot, own, oth)


def finish_kernel(
    plan_ref, parts_ref, back_c_ref, back_d_ref, grad_in_ref, grad_ref, total_ref, sems
):
    back = [back_c_ref.at[0], back_d_ref.at[0], back_d_ref.at[1]]
    copies = []
    for d in range(MOVES):
        s = plan_ref[LEAVES + d + 1]
        cp = pltpu.make_async_copy(back[d], grad_ref.at[jnp.maximum(s, 0)], sems.at[d])
        copies.append((s >= 0, cp))
    for moved, cp in copies:
        @pl.when(moved)
        def _(cp=cp):
            cp.start()

    n = parts_ref.shape[0]
    halves = []
    for c in range(2):
        total = parts_ref[c].astype(f32)
        for z in range(1, n // 2):
            total = total + parts_ref[2 * z + c].astype(f32)
        halves.append(total)
    total_ref[...] = jnp.concatenate(halves, axis=1)
    for moved, cp in copies:
        @pl.when(moved)
        def _(cp=cp):
            cp.wait()


def finish(plan, parts, back_c, back_d, grad):
    n, rows, half = parts.shape
    smem = pl.BlockSpec(memory_space=pltpu.SMEM)
    vmem = pl.BlockSpec(memory_space=pltpu.VMEM)
    hbm = pl.BlockSpec(memory_space=pl.ANY)
    return pl.pallas_call(
        finish_kernel,
        out_shape=(
            jax.ShapeDtypeStruct(grad.shape, bf16),
            jax.ShapeDtypeStruct((rows, 2 * half), f32),
        ),
        in_specs=[smem, vmem, vmem, vmem, hbm],
        out_specs=(hbm, vmem),
        scratch_shapes=[pltpu.SemaphoreType.DMA((MOVES,))],
        input_output_aliases={4: 0},
        compiler_params=pltpu.CompilerParams(vmem_limit_bytes=VMEM_LIMIT),
        name="finish",
    )(plan, parts, back_c, back_d, grad)


def shards(
    activations, cotangent, window_len, move_dest, move_slot, w_qkv, b_qkv, norm_gain, w_out
):
    n_shard = lax.axis_size("shard")
    rows = w_qkv.shape[0]
    tables = [t.transpose(2, 1, 0) for t in (window_len, move_dest, move_slot)]
    blob, par_a, par_b, plan = pack(
        tables, activations, w_qkv, b_qkv[None], norm_gain[None], w_out.T, n_shard
    )
    arr_a = permute_dp(par_a, 2)
    own = lax.all_to_all(blob, "shard", 0, 0)
    arr_b = permute_dp(jnp.stack([par_b, arr_a[1]]), 1)
    own, arr_b = lax.optimization_barrier((own, arr_b))
    oth = swap_cores(own)
    out, grad, ret_c, ret_d, gt_own, gt_oth = block(
        plan, activations, arr_a, arr_b, cotangent, own, oth
    )
    gt_in = swap_cores(gt_oth)
    back_c = permute_dp(ret_c, -1)
    share = (gt_own + gt_in.astype(f32)).astype(bf16).reshape(n_shard, rows, HALF)
    chunks = lax.all_to_all(share, "shard", 0, 0)
    summed = jnp.sum(chunks.astype(f32), axis=0).astype(bf16)
    back_d = permute_dp(jnp.stack([ret_d, back_c[1]]), -2)
    parts = lax.all_gather(summed, "dp", axis=0)
    grad_input, total = finish(plan, parts, back_c, back_d, grad)
    return (out, grad_input, total.T)


def solution(mesh):
    return jax.shard_map(
        shards,
        mesh=mesh,
        in_specs=(
            P(("dp", "shard"), None, None),
            P(("dp", "shard"), None, None),
            P(None, "shard", None),
            P(None, "shard", None),
            P(None, "shard", None),
            P("shard", None),
            P("shard"),
            P("shard"),
            P(None, "shard"),
        ),
        out_specs=(
            P(("dp", "shard"), None, None),
            P(("dp", "shard"), None, None),
            P(None, "shard"),
        ),
        check_vma=False,
    )
```

```python
import functools

import jax
import jax.numpy as jnp
from jax import lax
from jax.experimental import pallas as pl
from jax.experimental.pallas import tpu as pltpu
from jax.sharding import PartitionSpec as P

HEADS = 8
MOVES = 3
EPS = 1e-06
HALF = 320
PADH = 384
LANES = 128
CODES, LENS, STAYS, LEAVES, PLAN = 0, 16, 32, 48, 64
VMEM_LIMIT = 40 * 1024 * 1024
PACK_VMEM_LIMIT = 60 * 1024 * 1024

f32 = jnp.float32
bf16 = jnp.bfloat16


def permute_dp(array, by):
    n = lax.axis_size("dp")
    return lax.ppermute(array, "dp", [(i, (i + by) % n) for i in range(n)])


def swap_cores(array):
    n = lax.axis_size("dp")
    return lax.ppermute(array, "dp", [(i, i ^ 1) for i in range(n)])


def dot(a, b, ca, cb):
    return lax.dot_general(a, b, (((ca,), (cb,)), ((), ())), preferred_element_type=f32)


def tiles_of(groups):
    full = [g[:, t * LANES : (t + 1) * LANES] for g in groups for t in range(2)]
    half = [g[:, 2 * LANES : HALF] for g in groups]
    return full + [
        jnp.concatenate(half[0:2], axis=1),
        jnp.concatenate(half[2:4], axis=1),
    ]


def groups_of(tiles, rows):
    at = [tiles[t * rows : (t + 1) * rows] for t in range(10)]
    pad = jnp.zeros((rows, LANES // 2), f32)
    groups = []
    for g in range(4):
        both = at[8 + g // 2]
        half = both[:, (g % 2) * (LANES // 2) : (g % 2 + 1) * (LANES // 2)]
        groups.append(jnp.concatenate([at[2 * g], at[2 * g + 1], half, pad], axis=1))
    return groups


def share_tiles(x):
    low = x[0:24, 2 * LANES : HALF]
    high = jnp.concatenate([x[24:40, 2 * LANES : HALF], jnp.zeros((8, LANES // 2), f32)], axis=0)
    return jnp.concatenate(
        [x[:, 0:LANES], x[:, LANES : 2 * LANES], jnp.concatenate([low, high], axis=1)], axis=0
    )


def share_block(t):
    half = jnp.concatenate([t[80:104, 0 : LANES // 2], t[80:96, LANES // 2 :]], axis=0)
    return jnp.concatenate([t[0:40], t[40:80], half], axis=1)


SHARE = (104, LANES)


def pack_kernel(
    len_ref, dest_ref, slot_ref, act_ref, wqkv_ref, bias_ref, gain_ref, wout_ref,
    blob_ref, par_a_ref, par_b_ref, plan_ref, stage, sems, blob_sems,
):
    slots, _, n_dp = len_ref.shape
    n_shard = blob_ref.shape[0]
    inner = wout_ref.shape[1]
    me = lax.axis_index("dp")
    core = lax.rem(me, 2)
    for i in range(plan_ref.shape[0]):
        plan_ref[i] = 0 if LENS <= i < STAYS else -1
    for s in range(slots):
        live = len_ref[s, 0, me] > 0
        dest = dest_ref[s, 0, me]

        @pl.when(live & (dest == me))
        def _(s=s):
            b = slot_ref[s, 0, me]
            plan_ref[CODES + b] = s
            plan_ref[LENS + b] = len_ref[s, 0, me]
            plan_ref[STAYS + s] = b

        for d in range(1, MOVES + 1):
            @pl.when(live & (dest == lax.rem(me + d, n_dp)))
            def _(d=d, s=s):
                plan_ref[LEAVES + d] = s

    leaving = [
        pltpu.make_async_copy(
            act_ref.at[jnp.maximum(plan_ref[LEAVES + d], 0)], to, sems.at[d - 1]
        )
        for d, to in ((1, par_b_ref), (2, par_a_ref.at[0]), (3, par_a_ref.at[1]))
    ]
    for cp in leaving:
        cp.start()

    tail = [
        jnp.pad(r[...].astype(f32), ((0, 0), (0, LANES - r.shape[1])))
        for r in (bias_ref, gain_ref)
    ] + [jnp.zeros((6, LANES), f32)]
    for c in range(2):
        @pl.when(core == c)
        def _(c=c):
            groups = [
                wqkv_ref[:, g * inner + c * HALF : g * inner + (c + 1) * HALF].astype(f32)
                for g in range(3)
            ] + [wout_ref[:, c * HALF : (c + 1) * HALF].astype(f32)]
            stage[...] = jnp.concatenate(tiles_of(groups) + tail, axis=0).astype(bf16)
    copies = [
        pltpu.make_async_copy(stage, blob_ref.at[s], blob_sems.at[s]) for s in range(n_shard)
    ]
    for cp in copies:
        cp.start()

    for d in range(1, MOVES + 1):
        row = lax.rem(me - d + n_dp, n_dp)
        for s in range(slots):
            @pl.when((len_ref[s, 0, row] > 0) & (dest_ref[s, 0, row] == me))
            def _(d=d, s=s, row=row):
                b = slot_ref[s, 0, row]
                plan_ref[CODES + b] = slots + d - 1
                plan_ref[LENS + b] = len_ref[s, 0, row]

    for cp in leaving:
        cp.wait()
    for cp in copies:
        cp.wait()


def pack(tables, act, wqkv, bias, gain, wout_t, n_shard):
    rows = wqkv.shape[0]
    block_rows = 10 * rows + 8
    window = act.shape[1:]
    smem = pl.BlockSpec(memory_space=pltpu.SMEM)
    vmem = pl.BlockSpec(memory_space=pltpu.VMEM)
    hbm = pl.BlockSpec(memory_space=pl.ANY)
    return pl.pallas_call(
        pack_kernel,
        out_shape=(
            jax.ShapeDtypeStruct((n_shard, block_rows, LANES), bf16),
            jax.ShapeDtypeStruct((2,) + window, bf16),
            jax.ShapeDtypeStruct(window, bf16),
            jax.ShapeDtypeStruct((PLAN,), jnp.int32),
        ),
        in_specs=[smem, smem, smem, hbm, vmem, vmem, vmem, vmem],
        out_specs=(hbm, vmem, vmem, smem),
        scratch_shapes=[
            pltpu.VMEM((block_rows, LANES), bf16),
            pltpu.SemaphoreType.DMA((MOVES,)),
            pltpu.SemaphoreType.DMA((n_shard,)),
        ],
        compiler_params=pltpu.CompilerParams(vmem_limit_bytes=PACK_VMEM_LIMIT),
        name="pack_weights",
    )(*tables, act, wqkv, bias, gain, wout_t)


def unpack_weights(g, wqkv, wo, bias_row, gain_row):
    n_shard = g.shape[0]
    rows = g.shape[1] // 10
    for s in range(n_shard):
        tail = g[s].astype(f32)[10 * rows :]
        bias_row[0:1, 3 * rows * s : 3 * rows * (s + 1)] = tail[0:1, 0 : 3 * rows]
        gain_row[0:1, rows * s : rows * (s + 1)] = tail[1:2, 0:rows]
    for t in range(n_shard // 2):
        pair = [groups_of(g[2 * t + i].astype(f32), rows) for i in range(2)]
        at = pl.ds(2 * rows * t, 2 * rows)
        for k in range(4):
            piece = jnp.concatenate([pair[0][k], pair[1][k]], axis=0).astype(bf16)
            if k < 3:
                wqkv[at, k * PADH : (k + 1) * PADH] = piece
            else:
                wo[at, :] = piece


def bias_of(bias_row, low_half):
    parts = []
    for k in range(3):
        low = bias_row[0:1, 2 * k * HALF : (2 * k + 1) * HALF]
        high = bias_row[0:1, (2 * k + 1) * HALF : (2 * k + 2) * HALF]
        parts += [jnp.where(low_half, low, high), jnp.zeros((1, PADH - HALF), f32)]
    return jnp.concatenate(parts, axis=1)


def attention(lens, patches, qkv, da, att, dproj):
    head = HALF // 4
    scale = head ** (-0.5)
    starts = (0, LANES)
    lane = lax.broadcasted_iota(jnp.int32, (patches, 2 * LANES), 1)
    masks = []
    for i in range(4):
        low = i * head - starts[i // 2]
        masks.append(((lane >= low) & (lane < low + head)).astype(f32).astype(bf16))
    key_pos = lax.broadcasted_iota(jnp.int32, (patches, 2 * patches), 0)

    def by_head(m, g):
        return jnp.concatenate([m * masks[2 * g], m * masks[2 * g + 1]], axis=0)

    def joined(a, b):
        return jnp.concatenate(
            [a[:, :LANES], a[:, LANES:] + b[:, :LANES], b[:, LANES:]], axis=1
        ).astype(bf16)

    def stacked(m):
        return jnp.concatenate([m[:, :patches], m[:, patches:]], axis=0)

    def scored(w, g):
        at = pl.ds(w * patches, patches)
        low = starts[g]
        q, k, v = [qkv[at, i * PADH + low : i * PADH + low + 2 * LANES] for i in range(3)]
        q_heads = by_head(q, g)
        d_heads = by_head(da[at, low : low + 2 * LANES], g)
        return q_heads, d_heads, k, v, dot(k, q_heads, 1, 1), dot(v, d_heads, 1, 1)

    def softmaxed(w, g, q_heads, d_heads, k, v, scores, d_probs):
        allowed = key_pos < jnp.maximum(lens[w], 1)
        weights = jnp.where(allowed, jnp.exp(scores * scale), 0.0)
        probs = weights * (1.0 / jnp.sum(weights, axis=0, keepdims=True))
        d_probs = d_probs.astype(bf16).astype(f32)
        mean = jnp.sum(d_probs * probs, axis=0, keepdims=True)
        d_scores = (probs * (d_probs - mean) * scale).astype(bf16)
        return q_heads, d_heads, k, v, probs.astype(bf16), d_scores

    def combined(w, g, q_heads, d_heads, k, v, probs, d_scores):
        return (
            dot(stacked(probs), by_head(v, g), 0, 0),
            dot(stacked(d_scores), by_head(k, g), 0, 0),
            dot(d_scores, q_heads, 1, 0),
            dot(probs, d_heads, 1, 0),
        )

    todo = [(w, g) for w in range(len(lens)) for g in range(2)]
    step = 14
    for first in range(0, len(todo), step):
        some = todo[first : first + step]
        state = [scored(*p) for p in some]
        state = [softmaxed(*p, *c) for p, c in zip(some, state)]
        state = [combined(*p, *c) for p, c in zip(some, state)]
        for i in range(0, len(some), 2):
            at = pl.ds(some[i][0] * patches, patches)
            o, dq, dk, dv = [joined(x, y) for x, y in zip(state[i], state[i + 1])]
            att[at, :] = o
            dproj[at, 0:PADH] = dq
            dproj[at, PADH : 2 * PADH] = dk
            dproj[at, 2 * PADH :] = dv


def first_half_kernel(
    plan_ref, act_ref, arr_a_ref, arr_b_ref, cot_ref, g_ref,
    x_ref, nrm_ref, ub_ref, added_ref, dn_ref, gt_ref,
    xb, cotb, bias_row, gain_row, nrm, ub, wqkv, wo, qkv, da, att, dproj, added, dn, gt,
    win_sems, sems,
):
    slots = act_ref.shape[0]
    kept, patches, ch = xb.shape
    n_shard = g_ref.shape[0]
    rows = g_ref.shape[1] // 10
    core = lax.rem(lax.axis_index("dp"), 2)
    cot_copy = pltpu.make_async_copy(cot_ref, cotb, sems.at[0])
    cot_copy.start()
    xb[...] = jnp.zeros(xb.shape, bf16)
    code = [plan_ref[CODES + b] for b in range(kept)]
    lens = [plan_ref[LENS + b] for b in range(kept)]
    arrived = [arr_b_ref.at[0], arr_a_ref.at[0], arr_b_ref.at[1]]
    for b in range(kept):
        @pl.when((code[b] >= 0) & (code[b] < slots))
        def _(b=b):
            pltpu.make_async_copy(act_ref.at[code[b]], xb.at[b], win_sems.at[b]).start()

        for d in range(MOVES):
            @pl.when(code[b] == slots + d)
            def _(b=b, d=d):
                pltpu.make_async_copy(arrived[d], xb.at[b], win_sems.at[b]).start()

    unpack_weights(g_ref, wqkv, wo, bias_row, gain_row)
    bias = bias_of(bias_row, core == 0)
    gain = gain_row[...]
    cot_copy.wait()
    position = lax.broadcasted_iota(jnp.int32, (patches, 1), 0)
    for b in range(kept):
        @pl.when(code[b] >= 0)
        def _(b=b):
            pltpu.make_async_copy(act_ref.at[0], xb.at[b], win_sems.at[b]).wait()

        x = xb[b].astype(f32)
        inv = lax.rsqrt(jnp.mean(x * x, axis=-1, keepdims=True) + EPS)
        at = pl.ds(b * patches, patches)
        nrm[at, :] = (x * inv * gain).astype(bf16)
        ub[at, :] = jnp.where(position < lens[b], cotb[b].astype(f32), 0.0).astype(bf16)
    out = [
        pltpu.make_async_copy(v, r, sems.at[i])
        for i, (v, r) in enumerate(
            [(xb, x_ref), (nrm, nrm_ref), (ub, ub_ref), (gt, gt_ref), (added, added_ref), (dn, dn_ref)]
        )
    ]
    for cp in out[0:3]:
        cp.start()

    qkv[...] = (dot(nrm[...], wqkv[...], 1, 0) + bias).astype(bf16)
    da[...] = dot(ub[...], wo[...], 1, 0).astype(bf16)
    attention(lens, patches, qkv, da, att, dproj)
    whole = dot(ub[...], att[...], 0, 0)
    for s in range(n_shard):
        gt[s] = share_tiles(whole[s * rows : (s + 1) * rows]).astype(bf16)
    out[3].start()
    added[...] = dot(att[...], wo[...], 1, 1)
    out[4].start()
    dn[...] = dot(dproj[...], wqkv[...], 1, 1)
    out[5].start()
    for cp in out:
        cp.wait()


def second_half_kernel(
    plan_ref, x_ref, nrm_ref, ub_ref, added_ref, dn_ref, g_ref,
    out_ref, grad_ref, ret_c_ref, ret_d_ref, gt_ref,
    xb, nrm, ub, added, dn, outb, gbuf, zeros, bias_row, gain_row, wqkv, wo, qkv, da, att, dproj, gt,
    in_sems, zero_sems, win_sems, sems,
):
    slots = grad_ref.shape[0]
    kept, patches, ch = xb.shape
    n_shard = g_ref.shape[0]
    rows = g_ref.shape[1] // 10
    core = lax.rem(lax.axis_index("dp"), 2)
    loads = [
        pltpu.make_async_copy(r, v, in_sems.at[i])
        for i, (r, v) in enumerate(
            [(nrm_ref, nrm), (ub_ref, ub), (x_ref, xb), (added_ref, added), (dn_ref, dn)]
        )
    ]
    for cp in loads:
        cp.start()
    zeros[...] = jnp.zeros(zeros.shape, bf16)
    code = [plan_ref[CODES + b] for b in range(kept)]
    lens = [plan_ref[LENS + b] for b in range(kept)]

    def zero_copy(s):
        return pltpu.make_async_copy(zeros, grad_ref.at[s], zero_sems.at[s])

    for s in range(slots):
        @pl.when(plan_ref[STAYS + s] < 0)
        def _(s=s):
            zero_copy(s).start()

    returned = [ret_c_ref.at[0], ret_d_ref, ret_c_ref.at[1]]

    def ready(b):
        @pl.when((code[b] >= 0) & (code[b] < slots))
        def _():
            pltpu.make_async_copy(gbuf.at[b], grad_ref.at[code[b]], win_sems.at[b]).start()

        for d in range(MOVES):
            @pl.when(code[b] == slots + d)
            def _(d=d):
                pltpu.make_async_copy(gbuf.at[b], returned[d], win_sems.at[b]).start()

    unpack_weights(g_ref, wqkv, wo, bias_row, gain_row)
    bias = bias_of(bias_row, core == 1)
    gain = gain_row[...]
    loads[0].wait()
    loads[1].wait()
    qkv[...] = (dot(nrm[...], wqkv[...], 1, 0) + bias).astype(bf16)
    da[...] = dot(ub[...], wo[...], 1, 0).astype(bf16)
    attention(lens, patches, qkv, da, att, dproj)
    whole = dot(ub[...], att[...], 0, 0)
    for s in range(n_shard):
        gt[s] = share_tiles(whole[s * rows : (s + 1) * rows])
    gt_copy = pltpu.make_async_copy(gt, gt_ref, sems.at[0])
    gt_copy.start()
    for cp in loads[2:]:
        cp.wait()
    position = lax.broadcasted_iota(jnp.int32, (patches, 1), 0)
    total = added[...] + dot(att[...], wo[...], 1, 1)
    for b in range(kept):
        at = slice(b * patches, (b + 1) * patches)
        outb[b] = jnp.where(position < lens[b], xb[b].astype(f32) + total[at], 0.0).astype(bf16)
    out_copy = pltpu.make_async_copy(outb, out_ref, sems.at[1])
    out_copy.start()
    d_nrm = dn[...] + dot(dproj[...], wqkv[...], 1, 1)
    for b in range(kept):
        at = slice(b * patches, (b + 1) * patches)
        x = xb[b].astype(f32)
        inv = lax.rsqrt(jnp.mean(x * x, axis=-1, keepdims=True) + EPS)
        t = d_nrm[at].astype(bf16).astype(f32) * gain
        along = jnp.mean(t * x, axis=-1, keepdims=True)
        dx = t * inv - x * (inv * inv * inv * along)
        gbuf[b] = (ub[at, :].astype(f32) + dx).astype(bf16)
        ready(b)

    for b in range(kept):
        @pl.when(code[b] >= 0)
        def _(b=b):
            pltpu.make_async_copy(gbuf.at[b], grad_ref.at[0], win_sems.at[b]).wait()
    for s in range(slots):
        @pl.when(plan_ref[STAYS + s] < 0)
        def _(s=s):
            zero_copy(s).wait()
    gt_copy.wait()
    out_copy.wait()


def half_cost(tokens, patches, ch):
    work = 2 * tokens * HALF * (9 * ch + 6 * patches)
    return pl.CostEstimate(flops=work, bytes_accessed=8 * 1024 * 1024, transcendentals=4 * tokens * patches)


def half_scratch(tokens, ch):
    return [
        pltpu.VMEM((ch, 3 * PADH), bf16),
        pltpu.VMEM((ch, PADH), bf16),
        pltpu.VMEM((tokens, 3 * PADH), bf16),
        pltpu.VMEM((tokens, PADH), bf16),
        pltpu.VMEM((tokens, PADH), bf16),
        pltpu.VMEM((tokens, 3 * PADH), bf16),
    ]


def first_half(plan, act, arr_a, arr_b, cot, own):
    kept, patches, ch = cot.shape
    tokens = kept * patches
    share = (own.shape[0],) + SHARE
    smem = pl.BlockSpec(memory_space=pltpu.SMEM)
    vmem = pl.BlockSpec(memory_space=pltpu.VMEM)
    hbm = pl.BlockSpec(memory_space=pl.ANY)
    row = pltpu.VMEM((1, ch), f32)
    wide = pltpu.VMEM((tokens, ch), f32)
    narrow = pltpu.VMEM((tokens, ch), bf16)
    return pl.pallas_call(
        first_half_kernel,
        out_shape=(
            jax.ShapeDtypeStruct(cot.shape, bf16),
            jax.ShapeDtypeStruct((tokens, ch), bf16),
            jax.ShapeDtypeStruct((tokens, ch), bf16),
            jax.ShapeDtypeStruct((tokens, ch), f32),
            jax.ShapeDtypeStruct((tokens, ch), f32),
            jax.ShapeDtypeStruct(share, bf16),
        ),
        in_specs=[smem] + [hbm] * 4 + [vmem],
        out_specs=(hbm,) * 6,
        scratch_shapes=[
            pltpu.VMEM(cot.shape, bf16),
            pltpu.VMEM(cot.shape, bf16),
            pltpu.VMEM((1, 6 * HALF), f32),
            row, narrow, narrow,
            *half_scratch(tokens, ch),
            wide, wide,
            pltpu.VMEM(share, bf16),
            pltpu.SemaphoreType.DMA((kept,)),
            pltpu.SemaphoreType.DMA((6,)),
        ],
        compiler_params=pltpu.CompilerParams(vmem_limit_bytes=VMEM_LIMIT),
        cost_estimate=half_cost(tokens, patches, ch),
        name="first_half",
    )(plan, act, arr_a, arr_b, cot, own)


def second_half(plan, x, nrm, ub, added, dn, oth, slots):
    kept, patches, ch = x.shape
    tokens = kept * patches
    share = (oth.shape[0],) + SHARE
    window = (patches, ch)
    smem = pl.BlockSpec(memory_space=pltpu.SMEM)
    vmem = pl.BlockSpec(memory_space=pltpu.VMEM)
    hbm = pl.BlockSpec(memory_space=pl.ANY)
    row = pltpu.VMEM((1, ch), f32)
    wide = pltpu.VMEM((tokens, ch), f32)
    narrow = pltpu.VMEM((tokens, ch), bf16)
    held = pltpu.VMEM(x.shape, bf16)
    return pl.pallas_call(
        second_half_kernel,
        out_shape=(
            jax.ShapeDtypeStruct(x.shape, bf16),
            jax.ShapeDtypeStruct((slots,) + window, bf16),
            jax.ShapeDtypeStruct((2,) + window, bf16),
            jax.ShapeDtypeStruct(window, bf16),
            jax.ShapeDtypeStruct(share, f32),
        ),
        in_specs=[smem] + [hbm] * 5 + [vmem],
        out_specs=(hbm,) * 5,
        scratch_shapes=[
            held, narrow, narrow, wide, wide, held, held,
            pltpu.VMEM(window, bf16),
            pltpu.VMEM((1, 6 * HALF), f32),
            row,
            *half_scratch(tokens, ch),
            pltpu.VMEM(share, f32),
            pltpu.SemaphoreType.DMA((5,)),
            pltpu.SemaphoreType.DMA((slots,)),
            pltpu.SemaphoreType.DMA((kept,)),
            pltpu.SemaphoreType.DMA((2,)),
        ],
        compiler_params=pltpu.CompilerParams(vmem_limit_bytes=VMEM_LIMIT),
        cost_estimate=half_cost(tokens, patches, ch),
        name="second_half",
    )(plan, x, nrm, ub, added, dn, oth)


def finish_kernel(
    plan_ref, parts_ref, back_c_ref, back_d_ref, grad_in_ref, grad_ref, total_ref, sems
):
    back = [back_c_ref.at[0], back_d_ref.at[0], back_d_ref.at[1]]
    copies = []
    for d in range(MOVES):
        s = plan_ref[LEAVES + d + 1]
        cp = pltpu.make_async_copy(back[d], grad_ref.at[jnp.maximum(s, 0)], sems.at[d])
        copies.append((s >= 0, cp))
    for moved, cp in copies:
        @pl.when(moved)
        def _(cp=cp):
            cp.start()

    n = parts_ref.shape[0]
    halves = []
    for h in range(2):
        total = parts_ref[1 - h].astype(f32)
        for z in range(1, n // 2):
            total = total + parts_ref[2 * z + 1 - h].astype(f32)
        halves.append(share_block(total))
    total_ref[...] = jnp.concatenate(halves, axis=1)
    for moved, cp in copies:
        @pl.when(moved)
        def _(cp=cp):
            cp.wait()


def finish(plan, parts, back_c, back_d, grad, rows):
    smem = pl.BlockSpec(memory_space=pltpu.SMEM)
    vmem = pl.BlockSpec(memory_space=pltpu.VMEM)
    hbm = pl.BlockSpec(memory_space=pl.ANY)
    return pl.pallas_call(
        finish_kernel,
        out_shape=(
            jax.ShapeDtypeStruct(grad.shape, bf16),
            jax.ShapeDtypeStruct((rows, 2 * HALF), f32),
        ),
        in_specs=[smem, vmem, vmem, vmem, hbm],
        out_specs=(hbm, vmem),
        scratch_shapes=[pltpu.SemaphoreType.DMA((MOVES,))],
        input_output_aliases={4: 0},
        compiler_params=pltpu.CompilerParams(vmem_limit_bytes=VMEM_LIMIT),
        name="finish",
    )(plan, parts, back_c, back_d, grad)


def shards(
    activations, cotangent, window_len, move_dest, move_slot, w_qkv, b_qkv, norm_gain, w_out
):
    n_shard = lax.axis_size("shard")
    rows = w_qkv.shape[0]
    tables = [t.transpose(2, 1, 0) for t in (window_len, move_dest, move_slot)]
    blob, par_a, par_b, plan = pack(
        tables, activations, w_qkv, b_qkv[None], norm_gain[None], w_out.T, n_shard
    )
    arr_a = permute_dp(par_a, 2)
    own = lax.all_to_all(blob, "shard", 0, 0)
    arr_b = permute_dp(jnp.stack([par_b, arr_a[1]]), 1)
    own, arr_b = lax.optimization_barrier((own, arr_b))
    oth = swap_cores(own)
    x, nrm, ub, added, dn, gt_out = first_half(
        plan, activations, arr_a, arr_b, cotangent, own
    )
    gt_in = swap_cores(gt_out)
    out, grad, ret_c, ret_d, gt = second_half(
        plan, x, nrm, ub, added, dn, oth, activations.shape[0]
    )
    back_c = permute_dp(ret_c, -1)
    share = (gt + gt_in.astype(f32)).astype(bf16)
    chunks = lax.all_to_all(share, "shard", 0, 0)
    summed = jnp.sum(chunks.astype(f32), axis=0).astype(bf16)
    back_d = permute_dp(jnp.stack([ret_d, back_c[1]]), -2)
    parts = lax.all_gather(summed, "dp", axis=0)
    grad_input, total = finish(plan, parts, back_c, back_d, grad, rows)
    return (out, grad_input, total.T)


def solution(mesh):
    return jax.shard_map(
        shards,
        mesh=mesh,
        in_specs=(
            P(("dp", "shard"), None, None),
            P(("dp", "shard"), None, None),
            P(None, "shard", None),
            P(None, "shard", None),
            P(None, "shard", None),
            P("shard", None),
            P("shard"),
            P("shard"),
            P(None, "shard"),
        ),
        out_specs=(
            P(("dp", "shard"), None, None),
            P(("dp", "shard"), None, None),
            P(None, "shard"),
        ),
        check_vma=False,
    )
```

```python
import functools

import jax
import jax.numpy as jnp
from jax import lax
from jax.experimental import pallas as pl
from jax.experimental.pallas import tpu as pltpu
from jax.sharding import PartitionSpec as P

HEADS = 8
MOVES = 3
EPS = 1e-06
HALF = 320
PADH = 384
LANES = 128
KEPT = 7
CODES, LENS, STAYS, LEAVES, PLAN = 0, 16, 32, 48, 64
VMEM_LIMIT = 24 * 1024 * 1024
PACK_VMEM_LIMIT = 60 * 1024 * 1024

f32 = jnp.float32
bf16 = jnp.bfloat16


def permute_dp(array, by):
    n = lax.axis_size("dp")
    return lax.ppermute(array, "dp", [(i, (i + by) % n) for i in range(n)])


def swap_cores(array):
    n = lax.axis_size("dp")
    return lax.ppermute(array, "dp", [(i, i ^ 1) for i in range(n)])


def dot(a, b, ca, cb):
    return lax.dot_general(a, b, (((ca,), (cb,)), ((), ())), preferred_element_type=f32)


def tiles_of(groups):
    full = [g[:, t * LANES : (t + 1) * LANES] for g in groups for t in range(2)]
    half = [g[:, 2 * LANES : HALF] for g in groups]
    return full + [
        jnp.concatenate(half[0:2], axis=1),
        jnp.concatenate(half[2:4], axis=1),
    ]


def groups_of(tiles, rows):
    at = [tiles[t * rows : (t + 1) * rows] for t in range(10)]
    pad = jnp.zeros((rows, LANES // 2), f32)
    groups = []
    for g in range(4):
        both = at[8 + g // 2]
        half = both[:, (g % 2) * (LANES // 2) : (g % 2 + 1) * (LANES // 2)]
        groups.append(jnp.concatenate([at[2 * g], at[2 * g + 1], half, pad], axis=1))
    return groups


def share_tiles(x):
    low = x[0:24, 2 * LANES : HALF]
    high = jnp.concatenate([x[24:40, 2 * LANES : HALF], jnp.zeros((8, LANES // 2), f32)], axis=0)
    return jnp.concatenate(
        [x[:, 0:LANES], x[:, LANES : 2 * LANES], jnp.concatenate([low, high], axis=1)], axis=0
    )


def share_block(t):
    half = jnp.concatenate([t[80:104, 0 : LANES // 2], t[80:96, LANES // 2 :]], axis=0)
    return jnp.concatenate([t[0:40], t[40:80], half], axis=1)


SHARE = (104, LANES)


def pack_kernel(wqkv_ref, bias_ref, gain_ref, wout_ref, blob_ref, stage, sems):
    inner = wout_ref.shape[1]
    core = lax.rem(lax.axis_index("dp"), 2)
    tail = [
        jnp.pad(r[...].astype(f32), ((0, 0), (0, LANES - r.shape[1])))
        for r in (bias_ref, gain_ref)
    ] + [jnp.zeros((6, LANES), f32)]
    for c in range(2):
        @pl.when(core == c)
        def _(c=c):
            groups = [
                wqkv_ref[:, g * inner + c * HALF : g * inner + (c + 1) * HALF].astype(f32)
                for g in range(3)
            ] + [wout_ref[:, c * HALF : (c + 1) * HALF].astype(f32)]
            stage[...] = jnp.concatenate(tiles_of(groups) + tail, axis=0).astype(bf16)

    copies = [
        pltpu.make_async_copy(stage, blob_ref.at[s], sems.at[s]) for s in range(blob_ref.shape[0])
    ]
    for cp in copies:
        cp.start()
    for cp in copies:
        cp.wait()


def pack(wqkv, bias, gain, wout_t, n_shard):
    block_rows = 10 * wqkv.shape[0] + 8
    vmem = pl.BlockSpec(memory_space=pltpu.VMEM)
    hbm = pl.BlockSpec(memory_space=pl.ANY)
    return pl.pallas_call(
        pack_kernel,
        out_shape=jax.ShapeDtypeStruct((n_shard, block_rows, LANES), bf16),
        in_specs=[vmem] * 4,
        out_specs=hbm,
        scratch_shapes=[
            pltpu.VMEM((block_rows, LANES), bf16),
            pltpu.SemaphoreType.DMA((n_shard,)),
        ],
        compiler_params=pltpu.CompilerParams(vmem_limit_bytes=PACK_VMEM_LIMIT),
        name="pack_weights",
    )(wqkv, bias, gain, wout_t)


def plan_kernel(
    len_ref, dest_ref, slot_ref, act_ref, blob_ref, par_a_ref, par_b_ref, plan_ref, sems
):
    slots, _, n_dp = len_ref.shape
    me = lax.axis_index("dp")
    for i in range(plan_ref.shape[0]):
        plan_ref[i] = 0 if LENS <= i < STAYS else -1
    for s in range(slots):
        live = len_ref[s, 0, me] > 0
        dest = dest_ref[s, 0, me]

        @pl.when(live & (dest == me))
        def _(s=s):
            b = slot_ref[s, 0, me]
            plan_ref[CODES + b] = s
            plan_ref[LENS + b] = len_ref[s, 0, me]
            plan_ref[STAYS + s] = b

        for d in range(1, MOVES + 1):
            @pl.when(live & (dest == lax.rem(me + d, n_dp)))
            def _(d=d, s=s):
                plan_ref[LEAVES + d] = s

    leaving = [
        pltpu.make_async_copy(
            act_ref.at[jnp.maximum(plan_ref[LEAVES + d], 0)], to, sems.at[d - 1]
        )
        for d, to in ((1, par_b_ref), (2, par_a_ref.at[0]), (3, par_a_ref.at[1]))
    ]
    for cp in leaving:
        cp.start()
    for d in range(1, MOVES + 1):
        row = lax.rem(me - d + n_dp, n_dp)
        for s in range(slots):
            @pl.when((len_ref[s, 0, row] > 0) & (dest_ref[s, 0, row] == me))
            def _(d=d, s=s, row=row):
                b = slot_ref[s, 0, row]
                plan_ref[CODES + b] = slots + d - 1
                plan_ref[LENS + b] = len_ref[s, 0, row]

    for cp in leaving:
        cp.wait()


def make_plan(tables, act, blob):
    window = act.shape[1:]
    smem = pl.BlockSpec(memory_space=pltpu.SMEM)
    vmem = pl.BlockSpec(memory_space=pltpu.VMEM)
    hbm = pl.BlockSpec(memory_space=pl.ANY)
    return pl.pallas_call(
        plan_kernel,
        out_shape=(
            jax.ShapeDtypeStruct((2,) + window, bf16),
            jax.ShapeDtypeStruct(window, bf16),
            jax.ShapeDtypeStruct((PLAN,), jnp.int32),
        ),
        in_specs=[smem, smem, smem, hbm, hbm],
        out_specs=(vmem, vmem, smem),
        scratch_shapes=[pltpu.SemaphoreType.DMA((MOVES,))],
        compiler_params=pltpu.CompilerParams(vmem_limit_bytes=PACK_VMEM_LIMIT),
        cost_estimate=pl.CostEstimate(flops=0, bytes_accessed=4 * 1024 * 1024, transcendentals=0),
        name="make_plan",
    )(*tables, act, blob)


def arrange_kernel(
    plan_ref, act_ref, arr_a_ref, arr_b_ref, cot_ref, x_ref, scaled_ref, ub_ref, cotb, win_sems, sem
):
    slots = act_ref.shape[0]
    kept, patches, ch = x_ref.shape
    cot_copy = pltpu.make_async_copy(cot_ref, cotb, sem.at[0])
    cot_copy.start()
    code = [plan_ref[CODES + b] for b in range(kept)]
    arrived = [arr_b_ref.at[0], arr_a_ref.at[0], arr_b_ref.at[1]]
    for b in range(kept):
        @pl.when((code[b] >= 0) & (code[b] < slots))
        def _(b=b):
            pltpu.make_async_copy(act_ref.at[code[b]], x_ref.at[b], win_sems.at[b]).start()

        for d in range(MOVES):
            @pl.when(code[b] == slots + d)
            def _(b=b, d=d):
                pltpu.make_async_copy(arrived[d], x_ref.at[b], win_sems.at[b]).start()

        @pl.when(code[b] < 0)
        def _(b=b):
            x_ref[b] = jnp.zeros((patches, ch), bf16)

    cot_copy.wait()
    position = lax.broadcasted_iota(jnp.int32, (patches, 1), 0)
    for b in range(kept):
        live = position < plan_ref[LENS + b]
        ub_ref[b * patches : (b + 1) * patches, :] = jnp.where(
            live, cotb[b].astype(f32), 0.0
        ).astype(bf16)
    for b in range(kept):
        @pl.when(code[b] >= 0)
        def _(b=b):
            pltpu.make_async_copy(act_ref.at[0], x_ref.at[b], win_sems.at[b]).wait()

        x = x_ref[b].astype(f32)
        inv = lax.rsqrt(jnp.mean(x * x, axis=-1, keepdims=True) + EPS)
        scaled_ref[b * patches : (b + 1) * patches, :] = x * inv


def arrange(plan, act, arr_a, arr_b, cot):
    kept, patches, ch = cot.shape
    smem = pl.BlockSpec(memory_space=pltpu.SMEM)
    vmem = pl.BlockSpec(memory_space=pltpu.VMEM)
    hbm = pl.BlockSpec(memory_space=pl.ANY)
    return pl.pallas_call(
        arrange_kernel,
        out_shape=(
            jax.ShapeDtypeStruct(cot.shape, bf16),
            jax.ShapeDtypeStruct((kept * patches, ch), f32),
            jax.ShapeDtypeStruct((kept * patches, ch), bf16),
        ),
        in_specs=[smem] + [hbm] * 4,
        out_specs=(vmem,) * 3,
        scratch_shapes=[
            pltpu.VMEM(cot.shape, bf16),
            pltpu.SemaphoreType.DMA((kept,)),
            pltpu.SemaphoreType.DMA((1,)),
        ],
        compiler_params=pltpu.CompilerParams(vmem_limit_bytes=VMEM_LIMIT // 3),
        cost_estimate=pl.CostEstimate(flops=0, bytes_accessed=8 * 1024 * 1024, transcendentals=0),
        name="arrange_windows",
    )(plan, act, arr_a, arr_b, cot)


def unpack_weights(g, wqkv, wo, bias_row, gain_row):
    n_shard = g.shape[0]
    rows = g.shape[1] // 10
    for s in range(n_shard):
        tail = g[s].astype(f32)[10 * rows :]
        bias_row[0:1, 3 * rows * s : 3 * rows * (s + 1)] = tail[0:1, 0 : 3 * rows]
        gain_row[0:1, rows * s : rows * (s + 1)] = tail[1:2, 0:rows]
    for t in range(n_shard // 2):
        pair = [groups_of(g[2 * t + i].astype(f32), rows) for i in range(2)]
        at = pl.ds(2 * rows * t, 2 * rows)
        for k in range(4):
            piece = jnp.concatenate([pair[0][k], pair[1][k]], axis=0).astype(bf16)
            if k < 3:
                wqkv[at, k * PADH : (k + 1) * PADH] = piece
            else:
                wo[at, :] = piece


def bias_of(bias_row, low_half):
    parts = []
    for k in range(3):
        low = bias_row[0:1, 2 * k * HALF : (2 * k + 1) * HALF]
        high = bias_row[0:1, (2 * k + 1) * HALF : (2 * k + 2) * HALF]
        parts += [jnp.where(low_half, low, high), jnp.zeros((1, PADH - HALF), f32)]
    return jnp.concatenate(parts, axis=1)


def attention(lens, patches, qkv, da, att, dproj):
    head = HALF // 4
    scale = head ** (-0.5)
    starts = (0, LANES)
    lane = lax.broadcasted_iota(jnp.int32, (patches, 2 * LANES), 1)
    masks = []
    for i in range(4):
        low = i * head - starts[i // 2]
        masks.append(((lane >= low) & (lane < low + head)).astype(f32).astype(bf16))
    key_pos = lax.broadcasted_iota(jnp.int32, (patches, 2 * patches), 0)

    def by_head(m, g):
        return jnp.concatenate([m * masks[2 * g], m * masks[2 * g + 1]], axis=0)

    def joined(a, b):
        return jnp.concatenate(
            [a[:, :LANES], a[:, LANES:] + b[:, :LANES], b[:, LANES:]], axis=1
        ).astype(bf16)

    def stacked(m):
        return jnp.concatenate([m[:, :patches], m[:, patches:]], axis=0)

    def scored(w, g):
        at = pl.ds(w * patches, patches)
        low = starts[g]
        q, k, v = [qkv[at, i * PADH + low : i * PADH + low + 2 * LANES] for i in range(3)]
        q_heads = by_head(q, g)
        d_heads = by_head(da[at, low : low + 2 * LANES], g)
        return q_heads, d_heads, k, v, dot(k, q_heads, 1, 1), dot(v, d_heads, 1, 1)

    def softmaxed(w, g, q_heads, d_heads, k, v, scores, d_probs):
        allowed = key_pos < jnp.maximum(lens[w], 1)
        weights = jnp.where(allowed, jnp.exp(scores * scale), 0.0)
        probs = weights * (1.0 / jnp.sum(weights, axis=0, keepdims=True))
        d_probs = d_probs.astype(bf16).astype(f32)
        mean = jnp.sum(d_probs * probs, axis=0, keepdims=True)
        d_scores = (probs * (d_probs - mean) * scale).astype(bf16)
        return q_heads, d_heads, k, v, probs.astype(bf16), d_scores

    def combined(w, g, q_heads, d_heads, k, v, probs, d_scores):
        return (
            dot(stacked(probs), by_head(v, g), 0, 0),
            dot(stacked(d_scores), by_head(k, g), 0, 0),
            dot(d_scores, q_heads, 1, 0),
            dot(probs, d_heads, 1, 0),
        )

    todo = [(w, g) for w in range(len(lens)) for g in range(2)]
    step = 14
    for first in range(0, len(todo), step):
        some = todo[first : first + step]
        state = [scored(*p) for p in some]
        state = [softmaxed(*p, *c) for p, c in zip(some, state)]
        state = [combined(*p, *c) for p, c in zip(some, state)]
        for i in range(0, len(some), 2):
            at = pl.ds(some[i][0] * patches, patches)
            o, dq, dk, dv = [joined(x, y) for x, y in zip(state[i], state[i + 1])]
            att[at, :] = o
            dproj[at, 0:PADH] = dq
            dproj[at, PADH : 2 * PADH] = dk
            dproj[at, 2 * PADH :] = dv


def first_half_kernel(
    plan_ref, scaled, ub, g_ref, nrm, added, dn, gt,
    bias_row, gain_row, wqkv, wo, qkv, da, att, dproj,
):
    tokens = scaled.shape[0]
    patches = tokens // KEPT
    n_shard = g_ref.shape[0]
    rows = g_ref.shape[1] // 10
    core = lax.rem(lax.axis_index("dp"), 2)
    lens = [plan_ref[LENS + b] for b in range(KEPT)]
    unpack_weights(g_ref, wqkv, wo, bias_row, gain_row)
    bias = bias_of(bias_row, core == 0)
    nrm[...] = (scaled[...] * gain_row[...]).astype(bf16)
    qkv[...] = (dot(nrm[...], wqkv[...], 1, 0) + bias).astype(bf16)
    da[...] = dot(ub[...], wo[...], 1, 0).astype(bf16)
    attention(lens, patches, qkv, da, att, dproj)
    whole = dot(ub[...], att[...], 0, 0)
    for s in range(n_shard):
        gt[s] = share_tiles(whole[s * rows : (s + 1) * rows]).astype(bf16)
    added[...] = dot(att[...], wo[...], 1, 1)
    dn[...] = dot(dproj[...], wqkv[...], 1, 1)


def second_half_kernel(
    plan_ref, xb, nrm, ub, added, dn, g_ref,
    out_ref, grad_ref, ret_c_ref, ret_d_ref, gt,
    outb, gbuf, zeros, bias_row, gain_row, wqkv, wo, qkv, da, att, dproj,
    zero_sems, win_sems, out_sem,
):
    slots = grad_ref.shape[0]
    kept, patches, ch = xb.shape
    n_shard = g_ref.shape[0]
    rows = g_ref.shape[1] // 10
    core = lax.rem(lax.axis_index("dp"), 2)
    zeros[...] = jnp.zeros(zeros.shape, bf16)
    code = [plan_ref[CODES + b] for b in range(kept)]
    lens = [plan_ref[LENS + b] for b in range(kept)]

    def zero_copy(s):
        return pltpu.make_async_copy(zeros, grad_ref.at[s], zero_sems.at[s])

    for s in range(slots):
        @pl.when(plan_ref[STAYS + s] < 0)
        def _(s=s):
            zero_copy(s).start()

    returned = [ret_c_ref.at[0], ret_d_ref, ret_c_ref.at[1]]

    def ready(b):
        @pl.when((code[b] >= 0) & (code[b] < slots))
        def _():
            pltpu.make_async_copy(gbuf.at[b], grad_ref.at[code[b]], win_sems.at[b]).start()

        for d in range(MOVES):
            @pl.when(code[b] == slots + d)
            def _(d=d):
                pltpu.make_async_copy(gbuf.at[b], returned[d], win_sems.at[b]).start()

    unpack_weights(g_ref, wqkv, wo, bias_row, gain_row)
    bias = bias_of(bias_row, core == 1)
    gain = gain_row[...]
    qkv[...] = (dot(nrm[...], wqkv[...], 1, 0) + bias).astype(bf16)
    da[...] = dot(ub[...], wo[...], 1, 0).astype(bf16)
    attention(lens, patches, qkv, da, att, dproj)
    whole = dot(ub[...], att[...], 0, 0)
    for s in range(n_shard):
        gt[s] = share_tiles(whole[s * rows : (s + 1) * rows])
    position = lax.broadcasted_iota(jnp.int32, (patches, 1), 0)
    total = added[...] + dot(att[...], wo[...], 1, 1)
    for b in range(kept):
        at = slice(b * patches, (b + 1) * patches)
        outb[b] = jnp.where(position < lens[b], xb[b].astype(f32) + total[at], 0.0).astype(bf16)
    out_copy = pltpu.make_async_copy(outb, out_ref, out_sem.at[0])
    out_copy.start()
    d_nrm = dn[...] + dot(dproj[...], wqkv[...], 1, 1)
    for b in range(kept):
        at = slice(b * patches, (b + 1) * patches)
        x = xb[b].astype(f32)
        inv = lax.rsqrt(jnp.mean(x * x, axis=-1, keepdims=True) + EPS)
        t = d_nrm[at].astype(bf16).astype(f32) * gain
        along = jnp.mean(t * x, axis=-1, keepdims=True)
        dx = t * inv - x * (inv * inv * inv * along)
        gbuf[b] = (ub[at, :].astype(f32) + dx).astype(bf16)
        ready(b)

    for b in range(kept):
        @pl.when(code[b] >= 0)
        def _(b=b):
            pltpu.make_async_copy(gbuf.at[b], grad_ref.at[0], win_sems.at[b]).wait()
    for s in range(slots):
        @pl.when(plan_ref[STAYS + s] < 0)
        def _(s=s):
            zero_copy(s).wait()
    out_copy.wait()


def half_cost(tokens, patches, ch):
    work = 2 * tokens * HALF * (9 * ch + 6 * patches)
    return pl.CostEstimate(flops=work, bytes_accessed=8 * 1024 * 1024, transcendentals=4 * tokens * patches)


def half_scratch(tokens, ch):
    return [
        pltpu.VMEM((ch, 3 * PADH), bf16),
        pltpu.VMEM((ch, PADH), bf16),
        pltpu.VMEM((tokens, 3 * PADH), bf16),
        pltpu.VMEM((tokens, PADH), bf16),
        pltpu.VMEM((tokens, PADH), bf16),
        pltpu.VMEM((tokens, 3 * PADH), bf16),
    ]


def first_half(plan, scaled, ub, own):
    tokens, ch = scaled.shape
    share = (own.shape[0],) + SHARE
    smem = pl.BlockSpec(memory_space=pltpu.SMEM)
    vmem = pl.BlockSpec(memory_space=pltpu.VMEM)
    return pl.pallas_call(
        first_half_kernel,
        out_shape=(
            jax.ShapeDtypeStruct((tokens, ch), bf16),
            jax.ShapeDtypeStruct((tokens, ch), f32),
            jax.ShapeDtypeStruct((tokens, ch), f32),
            jax.ShapeDtypeStruct(share, bf16),
        ),
        in_specs=[smem, vmem, vmem, vmem],
        out_specs=(vmem,) * 4,
        scratch_shapes=[
            pltpu.VMEM((1, 6 * HALF), f32),
            pltpu.VMEM((1, ch), f32),
            *half_scratch(tokens, ch),
        ],
        compiler_params=pltpu.CompilerParams(vmem_limit_bytes=VMEM_LIMIT),
        cost_estimate=half_cost(tokens, tokens // KEPT, ch),
        name="first_half",
    )(plan, scaled, ub, own)


def second_half(plan, x, nrm, ub, added, dn, oth, slots):
    kept, patches, ch = x.shape
    tokens = kept * patches
    share = (oth.shape[0],) + SHARE
    window = (patches, ch)
    smem = pl.BlockSpec(memory_space=pltpu.SMEM)
    vmem = pl.BlockSpec(memory_space=pltpu.VMEM)
    hbm = pl.BlockSpec(memory_space=pl.ANY)
    held = pltpu.VMEM(x.shape, bf16)
    return pl.pallas_call(
        second_half_kernel,
        out_shape=(
            jax.ShapeDtypeStruct(x.shape, bf16),
            jax.ShapeDtypeStruct((slots,) + window, bf16),
            jax.ShapeDtypeStruct((2,) + window, bf16),
            jax.ShapeDtypeStruct(window, bf16),
            jax.ShapeDtypeStruct(share, f32),
        ),
        in_specs=[smem] + [vmem] * 6,
        out_specs=(hbm,) * 4 + (vmem,),
        scratch_shapes=[
            held, held,
            pltpu.VMEM(window, bf16),
            pltpu.VMEM((1, 6 * HALF), f32),
            pltpu.VMEM((1, ch), f32),
            *half_scratch(tokens, ch),
            pltpu.SemaphoreType.DMA((slots,)),
            pltpu.SemaphoreType.DMA((kept,)),
            pltpu.SemaphoreType.DMA((1,)),
        ],
        compiler_params=pltpu.CompilerParams(vmem_limit_bytes=VMEM_LIMIT),
        cost_estimate=half_cost(tokens, patches, ch),
        name="second_half",
    )(plan, x, nrm, ub, added, dn, oth)


def finish_kernel(
    plan_ref, parts_ref, back_c_ref, back_d_ref, grad_in_ref, grad_ref, total_ref, sems
):
    back = [back_c_ref.at[0], back_d_ref.at[0], back_d_ref.at[1]]
    copies = []
    for d in range(MOVES):
        s = plan_ref[LEAVES + d + 1]
        cp = pltpu.make_async_copy(back[d], grad_ref.at[jnp.maximum(s, 0)], sems.at[d])
        copies.append((s >= 0, cp))
    for moved, cp in copies:
        @pl.when(moved)
        def _(cp=cp):
            cp.start()

    n = parts_ref.shape[0]
    halves = []
    for h in range(2):
        total = parts_ref[1 - h].astype(f32)
        for z in range(1, n // 2):
            total = total + parts_ref[2 * z + 1 - h].astype(f32)
        halves.append(share_block(total))
    total_ref[...] = jnp.concatenate(halves, axis=1)
    for moved, cp in copies:
        @pl.when(moved)
        def _(cp=cp):
            cp.wait()


def finish(plan, parts, back_c, back_d, grad, rows):
    smem = pl.BlockSpec(memory_space=pltpu.SMEM)
    vmem = pl.BlockSpec(memory_space=pltpu.VMEM)
    hbm = pl.BlockSpec(memory_space=pl.ANY)
    return pl.pallas_call(
        finish_kernel,
        out_shape=(
            jax.ShapeDtypeStruct(grad.shape, bf16),
            jax.ShapeDtypeStruct((rows, 2 * HALF), f32),
        ),
        in_specs=[smem, vmem, vmem, vmem, hbm],
        out_specs=(hbm, vmem),
        scratch_shapes=[pltpu.SemaphoreType.DMA((MOVES,))],
        input_output_aliases={4: 0},
        compiler_params=pltpu.CompilerParams(vmem_limit_bytes=VMEM_LIMIT),
        name="finish",
    )(plan, parts, back_c, back_d, grad)


def shards(
    activations, cotangent, window_len, move_dest, move_slot, w_qkv, b_qkv, norm_gain, w_out
):
    n_shard = lax.axis_size("shard")
    rows = w_qkv.shape[0]
    tables = [t.transpose(2, 1, 0) for t in (window_len, move_dest, move_slot)]
    blob = pack(w_qkv, b_qkv[None], norm_gain[None], w_out.T, n_shard)
    own = lax.all_to_all(blob, "shard", 0, 0)
    par_a, par_b, plan = make_plan(tables, activations, blob)
    arr_a = permute_dp(par_a, 2)
    arr_b = permute_dp(jnp.stack([par_b, arr_a[1]]), 1)
    x, scaled, ub = arrange(plan, activations, arr_a, arr_b, cotangent)
    own, x, scaled, ub = lax.optimization_barrier((own, x, scaled, ub))
    oth = swap_cores(own)
    nrm, added, dn, gt_out = first_half(plan, scaled, ub, own)
    gt_in = swap_cores(gt_out)
    out, grad, ret_c, ret_d, gt = second_half(
        plan, x, nrm, ub, added, dn, oth, activations.shape[0]
    )
    back_c = permute_dp(ret_c, -1)
    share = (gt + gt_in.astype(f32)).astype(bf16)
    chunks = lax.all_to_all(share, "shard", 0, 0)
    summed = jnp.sum(chunks.astype(f32), axis=0).astype(bf16)
    back_d = permute_dp(jnp.stack([ret_d, back_c[1]]), -2)
    parts = lax.all_gather(summed, "dp", axis=0)
    grad_input, total = finish(plan, parts, back_c, back_d, grad, rows)
    return (out, grad_input, total.T)


def solution(mesh):
    return jax.shard_map(
        shards,
        mesh=mesh,
        in_specs=(
            P(("dp", "shard"), None, None),
            P(("dp", "shard"), None, None),
            P(None, "shard", None),
            P(None, "shard", None),
            P(None, "shard", None),
            P("shard", None),
            P("shard"),
            P("shard"),
            P(None, "shard"),
        ),
        out_specs=(
            P(("dp", "shard"), None, None),
            P(("dp", "shard"), None, None),
            P(None, "shard"),
        ),
        check_vma=False,
    )
```

```python
import functools

import jax
import jax.numpy as jnp
from jax import lax
from jax.experimental import pallas as pl
from jax.experimental.pallas import tpu as pltpu
from jax.sharding import PartitionSpec as P

HEADS = 8
MOVES = 3
EPS = 1e-06
HALF = 320
PADH = 384
LANES = 128
CODES, LENS, STAYS, LEAVES, PLAN = 0, 16, 32, 48, 64
VMEM_LIMIT = 24 * 1024 * 1024
PACK_VMEM_LIMIT = 60 * 1024 * 1024

f32 = jnp.float32
bf16 = jnp.bfloat16


def permute_dp(array, by):
    n = lax.axis_size("dp")
    return lax.ppermute(array, "dp", [(i, (i + by) % n) for i in range(n)])


def swap_cores(array):
    n = lax.axis_size("dp")
    return lax.ppermute(array, "dp", [(i, i ^ 1) for i in range(n)])


def dot(a, b, ca, cb):
    return lax.dot_general(a, b, (((ca,), (cb,)), ((), ())), preferred_element_type=f32)


def tiles_of(groups):
    full = [g[:, t * LANES : (t + 1) * LANES] for g in groups for t in range(2)]
    half = [g[:, 2 * LANES : HALF] for g in groups]
    return full + [
        jnp.concatenate(half[0:2], axis=1),
        jnp.concatenate(half[2:4], axis=1),
    ]


def groups_of(tiles, rows):
    at = [tiles[t * rows : (t + 1) * rows] for t in range(10)]
    pad = jnp.zeros((rows, LANES // 2), f32)
    groups = []
    for g in range(4):
        both = at[8 + g // 2]
        half = both[:, (g % 2) * (LANES // 2) : (g % 2 + 1) * (LANES // 2)]
        groups.append(jnp.concatenate([at[2 * g], at[2 * g + 1], half, pad], axis=1))
    return groups


def share_tiles(x):
    low = x[0:24, 2 * LANES : HALF]
    high = jnp.concatenate([x[24:40, 2 * LANES : HALF], jnp.zeros((8, LANES // 2), f32)], axis=0)
    return jnp.concatenate(
        [x[:, 0:LANES], x[:, LANES : 2 * LANES], jnp.concatenate([low, high], axis=1)], axis=0
    )


def share_block(t):
    half = jnp.concatenate([t[80:104, 0 : LANES // 2], t[80:96, LANES // 2 :]], axis=0)
    return jnp.concatenate([t[0:40], t[40:80], half], axis=1)


SHARE = (104, LANES)


def pack_kernel(wqkv_ref, bias_ref, gain_ref, wout_ref, blob_ref, stage, sems):
    inner = wout_ref.shape[1]
    core = lax.rem(lax.axis_index("dp"), 2)
    tail = [
        jnp.pad(r[...].astype(f32), ((0, 0), (0, LANES - r.shape[1])))
        for r in (bias_ref, gain_ref)
    ] + [jnp.zeros((6, LANES), f32)]
    for c in range(2):
        @pl.when(core == c)
        def _(c=c):
            groups = [
                wqkv_ref[:, g * inner + c * HALF : g * inner + (c + 1) * HALF].astype(f32)
                for g in range(3)
            ] + [wout_ref[:, c * HALF : (c + 1) * HALF].astype(f32)]
            stage[...] = jnp.concatenate(tiles_of(groups) + tail, axis=0).astype(bf16)

    copies = [
        pltpu.make_async_copy(stage, blob_ref.at[s], sems.at[s]) for s in range(blob_ref.shape[0])
    ]
    for cp in copies:
        cp.start()
    for cp in copies:
        cp.wait()


def pack(wqkv, bias, gain, wout_t, n_shard):
    block_rows = 10 * wqkv.shape[0] + 8
    vmem = pl.BlockSpec(memory_space=pltpu.VMEM)
    hbm = pl.BlockSpec(memory_space=pl.ANY)
    return pl.pallas_call(
        pack_kernel,
        out_shape=jax.ShapeDtypeStruct((n_shard, block_rows, LANES), bf16),
        in_specs=[vmem] * 4,
        out_specs=hbm,
        scratch_shapes=[
            pltpu.VMEM((block_rows, LANES), bf16),
            pltpu.SemaphoreType.DMA((n_shard,)),
        ],
        compiler_params=pltpu.CompilerParams(vmem_limit_bytes=PACK_VMEM_LIMIT),
        name="pack_weights",
    )(wqkv, bias, gain, wout_t)


def plan_kernel(
    len_ref, dest_ref, slot_ref, act_ref, blob_ref, par_a_ref, par_b_ref, plan_ref, sems
):
    slots, _, n_dp = len_ref.shape
    me = lax.axis_index("dp")
    for i in range(plan_ref.shape[0]):
        plan_ref[i] = 0 if LENS <= i < STAYS else -1
    for s in range(slots):
        live = len_ref[s, 0, me] > 0
        dest = dest_ref[s, 0, me]

        @pl.when(live & (dest == me))
        def _(s=s):
            b = slot_ref[s, 0, me]
            plan_ref[CODES + b] = s
            plan_ref[LENS + b] = len_ref[s, 0, me]
            plan_ref[STAYS + s] = b

        for d in range(1, MOVES + 1):
            @pl.when(live & (dest == lax.rem(me + d, n_dp)))
            def _(d=d, s=s):
                plan_ref[LEAVES + d] = s

    leaving = [
        pltpu.make_async_copy(
            act_ref.at[jnp.maximum(plan_ref[LEAVES + d], 0)], to, sems.at[d - 1]
        )
        for d, to in ((1, par_b_ref), (2, par_a_ref.at[0]), (3, par_a_ref.at[1]))
    ]
    for cp in leaving:
        cp.start()
    for d in range(1, MOVES + 1):
        row = lax.rem(me - d + n_dp, n_dp)
        for s in range(slots):
            @pl.when((len_ref[s, 0, row] > 0) & (dest_ref[s, 0, row] == me))
            def _(d=d, s=s, row=row):
                b = slot_ref[s, 0, row]
                plan_ref[CODES + b] = slots + d - 1
                plan_ref[LENS + b] = len_ref[s, 0, row]

    for cp in leaving:
        cp.wait()


def make_plan(tables, act, blob):
    window = act.shape[1:]
    smem = pl.BlockSpec(memory_space=pltpu.SMEM)
    vmem = pl.BlockSpec(memory_space=pltpu.VMEM)
    hbm = pl.BlockSpec(memory_space=pl.ANY)
    return pl.pallas_call(
        plan_kernel,
        out_shape=(
            jax.ShapeDtypeStruct((2,) + window, bf16),
            jax.ShapeDtypeStruct(window, bf16),
            jax.ShapeDtypeStruct((PLAN,), jnp.int32),
        ),
        in_specs=[smem, smem, smem, hbm, hbm],
        out_specs=(vmem, vmem, smem),
        scratch_shapes=[pltpu.SemaphoreType.DMA((MOVES,))],
        compiler_params=pltpu.CompilerParams(vmem_limit_bytes=PACK_VMEM_LIMIT),
        cost_estimate=pl.CostEstimate(flops=0, bytes_accessed=4 * 1024 * 1024, transcendentals=0),
        name="make_plan",
    )(*tables, act, blob)


def arrange_kernel(
    plan_ref, act_ref, arr_a_ref, arr_b_ref, cot_ref, x_ref, inv_ref, ub_ref, cotb, win_sems, sem
):
    slots = act_ref.shape[0]
    kept, patches, ch = x_ref.shape
    cot_copy = pltpu.make_async_copy(cot_ref, cotb, sem.at[0])
    cot_copy.start()
    code = [plan_ref[CODES + b] for b in range(kept)]
    arrived = [arr_b_ref.at[0], arr_a_ref.at[0], arr_b_ref.at[1]]
    for b in range(kept):
        @pl.when((code[b] >= 0) & (code[b] < slots))
        def _(b=b):
            pltpu.make_async_copy(act_ref.at[code[b]], x_ref.at[b], win_sems.at[b]).start()

        for d in range(MOVES):
            @pl.when(code[b] == slots + d)
            def _(b=b, d=d):
                pltpu.make_async_copy(arrived[d], x_ref.at[b], win_sems.at[b]).start()

        @pl.when(code[b] < 0)
        def _(b=b):
            x_ref[b] = jnp.zeros((patches, ch), bf16)

    cot_copy.wait()
    position = lax.broadcasted_iota(jnp.int32, (patches, 1), 0)
    for b in range(kept):
        live = position < plan_ref[LENS + b]
        ub_ref[b * patches : (b + 1) * patches, :] = jnp.where(
            live, cotb[b].astype(f32), 0.0
        ).astype(bf16)
    for b in range(kept):
        @pl.when(code[b] >= 0)
        def _(b=b):
            pltpu.make_async_copy(act_ref.at[0], x_ref.at[b], win_sems.at[b]).wait()

        x = x_ref[b].astype(f32)
        inv = lax.rsqrt(jnp.mean(x * x, axis=-1, keepdims=True) + EPS)
        inv_ref[b * patches : (b + 1) * patches, :] = jnp.broadcast_to(inv, (patches, LANES))


def arrange(plan, act, arr_a, arr_b, cot):
    kept, patches, ch = cot.shape
    smem = pl.BlockSpec(memory_space=pltpu.SMEM)
    vmem = pl.BlockSpec(memory_space=pltpu.VMEM)
    hbm = pl.BlockSpec(memory_space=pl.ANY)
    return pl.pallas_call(
        arrange_kernel,
        out_shape=(
            jax.ShapeDtypeStruct(cot.shape, bf16),
            jax.ShapeDtypeStruct((kept * patches, LANES), f32),
            jax.ShapeDtypeStruct((kept * patches, ch), bf16),
        ),
        in_specs=[smem] + [hbm] * 4,
        out_specs=(vmem,) * 3,
        scratch_shapes=[
            pltpu.VMEM(cot.shape, bf16),
            pltpu.SemaphoreType.DMA((kept,)),
            pltpu.SemaphoreType.DMA((1,)),
        ],
        compiler_params=pltpu.CompilerParams(vmem_limit_bytes=VMEM_LIMIT // 3),
        cost_estimate=pl.CostEstimate(flops=0, bytes_accessed=8 * 1024 * 1024, transcendentals=0),
        name="arrange_windows",
    )(plan, act, arr_a, arr_b, cot)


def unpack_weights(g, wqkv, wo, bias_row, gain_row):
    n_shard = g.shape[0]
    rows = g.shape[1] // 10
    for s in range(n_shard):
        tail = g[s].astype(f32)[10 * rows :]
        bias_row[0:1, 3 * rows * s : 3 * rows * (s + 1)] = tail[0:1, 0 : 3 * rows]
        gain_row[0:1, rows * s : rows * (s + 1)] = tail[1:2, 0:rows]
    for t in range(n_shard // 2):
        pair = [groups_of(g[2 * t + i].astype(f32), rows) for i in range(2)]
        at = pl.ds(2 * rows * t, 2 * rows)
        for k in range(4):
            piece = jnp.concatenate([pair[0][k], pair[1][k]], axis=0).astype(bf16)
            if k < 3:
                wqkv[at, k * PADH : (k + 1) * PADH] = piece
            else:
                wo[at, :] = piece


def bias_of(bias_row, low_half):
    parts = []
    for k in range(3):
        low = bias_row[0:1, 2 * k * HALF : (2 * k + 1) * HALF]
        high = bias_row[0:1, (2 * k + 1) * HALF : (2 * k + 2) * HALF]
        parts += [jnp.where(low_half, low, high), jnp.zeros((1, PADH - HALF), f32)]
    return jnp.concatenate(parts, axis=1)


def attention(lens, patches, qkv, da, att, dproj):
    head = HALF // 4
    scale = head ** (-0.5)
    starts = (0, LANES)
    lane = lax.broadcasted_iota(jnp.int32, (patches, 2 * LANES), 1)
    masks = []
    for i in range(4):
        low = i * head - starts[i // 2]
        masks.append(((lane >= low) & (lane < low + head)).astype(f32).astype(bf16))
    key_pos = lax.broadcasted_iota(jnp.int32, (patches, 2 * patches), 0)

    def by_head(m, g):
        return jnp.concatenate([m * masks[2 * g], m * masks[2 * g + 1]], axis=0)

    def joined(a, b):
        return jnp.concatenate(
            [a[:, :LANES], a[:, LANES:] + b[:, :LANES], b[:, LANES:]], axis=1
        ).astype(bf16)

    def stacked(m):
        return jnp.concatenate([m[:, :patches], m[:, patches:]], axis=0)

    def scored(w, g):
        at = pl.ds(w * patches, patches)
        low = starts[g]
        q, k, v = [qkv[at, i * PADH + low : i * PADH + low + 2 * LANES] for i in range(3)]
        q_heads = by_head(q, g)
        d_heads = by_head(da[at, low : low + 2 * LANES], g)
        return q_heads, d_heads, k, v, dot(k, q_heads, 1, 1), dot(v, d_heads, 1, 1)

    def softmaxed(w, g, q_heads, d_heads, k, v, scores, d_probs):
        allowed = key_pos < jnp.maximum(lens[w], 1)
        weights = jnp.where(allowed, jnp.exp(scores * scale), 0.0)
        probs = weights * (1.0 / jnp.sum(weights, axis=0, keepdims=True))
        d_probs = d_probs.astype(bf16).astype(f32)
        mean = jnp.sum(d_probs * probs, axis=0, keepdims=True)
        d_scores = (probs * (d_probs - mean) * scale).astype(bf16)
        return q_heads, d_heads, k, v, probs.astype(bf16), d_scores

    def combined(w, g, q_heads, d_heads, k, v, probs, d_scores):
        return (
            dot(stacked(probs), by_head(v, g), 0, 0),
            dot(stacked(d_scores), by_head(k, g), 0, 0),
            dot(d_scores, q_heads, 1, 0),
            dot(probs, d_heads, 1, 0),
        )

    todo = [(w, g) for w in range(len(lens)) for g in range(2)]
    step = 14
    for first in range(0, len(todo), step):
        some = todo[first : first + step]
        state = [scored(*p) for p in some]
        state = [softmaxed(*p, *c) for p, c in zip(some, state)]
        state = [combined(*p, *c) for p, c in zip(some, state)]
        for i in range(0, len(some), 2):
            at = pl.ds(some[i][0] * patches, patches)
            o, dq, dk, dv = [joined(x, y) for x, y in zip(state[i], state[i + 1])]
            att[at, :] = o
            dproj[at, 0:PADH] = dq
            dproj[at, PADH : 2 * PADH] = dk
            dproj[at, 2 * PADH :] = dv


def first_half_kernel(
    plan_ref, xb, inv_ref, ub, g_ref, nrm, added, dn, gt,
    bias_row, gain_row, wqkv, wo, qkv, da, att, dproj,
):
    kept, patches, ch = xb.shape
    n_shard = g_ref.shape[0]
    rows = g_ref.shape[1] // 10
    core = lax.rem(lax.axis_index("dp"), 2)
    lens = [plan_ref[LENS + b] for b in range(kept)]
    unpack_weights(g_ref, wqkv, wo, bias_row, gain_row)
    bias = bias_of(bias_row, core == 0)
    gain = gain_row[...]
    for b in range(kept):
        at = slice(b * patches, (b + 1) * patches)
        inv = jnp.concatenate([inv_ref[at, :]] * (ch // LANES), axis=1)
        nrm[at, :] = (xb[b].astype(f32) * inv * gain).astype(bf16)
    qkv[...] = (dot(nrm[...], wqkv[...], 1, 0) + bias).astype(bf16)
    da[...] = dot(ub[...], wo[...], 1, 0).astype(bf16)
    attention(lens, patches, qkv, da, att, dproj)
    whole = dot(ub[...], att[...], 0, 0)
    for s in range(n_shard):
        gt[s] = share_tiles(whole[s * rows : (s + 1) * rows]).astype(bf16)
    added[...] = dot(att[...], wo[...], 1, 1)
    dn[...] = dot(dproj[...], wqkv[...], 1, 1)


def second_half_kernel(
    plan_ref, xb, inv_ref, nrm, ub, added, dn, g_ref,
    out_ref, grad_ref, ret_c_ref, ret_d_ref, gt,
    outb, gbuf, zeros, bias_row, gain_row, wqkv, wo, qkv, da, att, dproj,
    zero_sems, win_sems, out_sem,
):
    slots = grad_ref.shape[0]
    kept, patches, ch = xb.shape
    n_shard = g_ref.shape[0]
    rows = g_ref.shape[1] // 10
    core = lax.rem(lax.axis_index("dp"), 2)
    zeros[...] = jnp.zeros(zeros.shape, bf16)
    code = [plan_ref[CODES + b] for b in range(kept)]
    lens = [plan_ref[LENS + b] for b in range(kept)]

    def zero_copy(s):
        return pltpu.make_async_copy(zeros, grad_ref.at[s], zero_sems.at[s])

    for s in range(slots):
        @pl.when(plan_ref[STAYS + s] < 0)
        def _(s=s):
            zero_copy(s).start()

    returned = [ret_c_ref.at[0], ret_d_ref, ret_c_ref.at[1]]

    def ready(b):
        @pl.when((code[b] >= 0) & (code[b] < slots))
        def _():
            pltpu.make_async_copy(gbuf.at[b], grad_ref.at[code[b]], win_sems.at[b]).start()

        for d in range(MOVES):
            @pl.when(code[b] == slots + d)
            def _(d=d):
                pltpu.make_async_copy(gbuf.at[b], returned[d], win_sems.at[b]).start()

    unpack_weights(g_ref, wqkv, wo, bias_row, gain_row)
    bias = bias_of(bias_row, core == 1)
    gain = gain_row[...]
    qkv[...] = (dot(nrm[...], wqkv[...], 1, 0) + bias).astype(bf16)
    da[...] = dot(ub[...], wo[...], 1, 0).astype(bf16)
    attention(lens, patches, qkv, da, att, dproj)
    whole = dot(ub[...], att[...], 0, 0)
    for s in range(n_shard):
        gt[s] = share_tiles(whole[s * rows : (s + 1) * rows])
    position = lax.broadcasted_iota(jnp.int32, (patches, 1), 0)
    total = added[...] + dot(att[...], wo[...], 1, 1)
    for b in range(kept):
        at = slice(b * patches, (b + 1) * patches)
        outb[b] = jnp.where(position < lens[b], xb[b].astype(f32) + total[at], 0.0).astype(bf16)
    out_copy = pltpu.make_async_copy(outb, out_ref, out_sem.at[0])
    out_copy.start()
    d_nrm = dn[...] + dot(dproj[...], wqkv[...], 1, 1)
    for b in range(kept):
        at = slice(b * patches, (b + 1) * patches)
        x = xb[b].astype(f32)
        inv = jnp.concatenate([inv_ref[at, :]] * (ch // LANES), axis=1)
        t = d_nrm[at].astype(bf16).astype(f32) * gain
        along = jnp.mean(t * x, axis=-1, keepdims=True)
        dx = t * inv - x * (inv * inv * inv * along)
        gbuf[b] = (ub[at, :].astype(f32) + dx).astype(bf16)
        ready(b)

    for b in range(kept):
        @pl.when(code[b] >= 0)
        def _(b=b):
            pltpu.make_async_copy(gbuf.at[b], grad_ref.at[0], win_sems.at[b]).wait()
    for s in range(slots):
        @pl.when(plan_ref[STAYS + s] < 0)
        def _(s=s):
            zero_copy(s).wait()
    out_copy.wait()


def half_cost(tokens, patches, ch):
    work = 2 * tokens * HALF * (9 * ch + 6 * patches)
    return pl.CostEstimate(flops=work, bytes_accessed=8 * 1024 * 1024, transcendentals=4 * tokens * patches)


def half_scratch(tokens, ch):
    return [
        pltpu.VMEM((ch, 3 * PADH), bf16),
        pltpu.VMEM((ch, PADH), bf16),
        pltpu.VMEM((tokens, 3 * PADH), bf16),
        pltpu.VMEM((tokens, PADH), bf16),
        pltpu.VMEM((tokens, PADH), bf16),
        pltpu.VMEM((tokens, 3 * PADH), bf16),
    ]


def first_half(plan, x, inv, ub, own):
    kept, patches, ch = x.shape
    tokens = kept * patches
    share = (own.shape[0],) + SHARE
    smem = pl.BlockSpec(memory_space=pltpu.SMEM)
    vmem = pl.BlockSpec(memory_space=pltpu.VMEM)
    return pl.pallas_call(
        first_half_kernel,
        out_shape=(
            jax.ShapeDtypeStruct((tokens, ch), bf16),
            jax.ShapeDtypeStruct((tokens, ch), f32),
            jax.ShapeDtypeStruct((tokens, ch), f32),
            jax.ShapeDtypeStruct(share, bf16),
        ),
        in_specs=[smem, vmem, vmem, vmem, vmem],
        out_specs=(vmem,) * 4,
        scratch_shapes=[
            pltpu.VMEM((1, 6 * HALF), f32),
            pltpu.VMEM((1, ch), f32),
            *half_scratch(tokens, ch),
        ],
        compiler_params=pltpu.CompilerParams(vmem_limit_bytes=VMEM_LIMIT),
        cost_estimate=half_cost(tokens, patches, ch),
        name="first_half",
    )(plan, x, inv, ub, own)


def second_half(plan, x, inv, nrm, ub, added, dn, oth, slots):
    kept, patches, ch = x.shape
    tokens = kept * patches
    share = (oth.shape[0],) + SHARE
    window = (patches, ch)
    smem = pl.BlockSpec(memory_space=pltpu.SMEM)
    vmem = pl.BlockSpec(memory_space=pltpu.VMEM)
    hbm = pl.BlockSpec(memory_space=pl.ANY)
    held = pltpu.VMEM(x.shape, bf16)
    return pl.pallas_call(
        second_half_kernel,
        out_shape=(
            jax.ShapeDtypeStruct(x.shape, bf16),
            jax.ShapeDtypeStruct((slots,) + window, bf16),
            jax.ShapeDtypeStruct((2,) + window, bf16),
            jax.ShapeDtypeStruct(window, bf16),
            jax.ShapeDtypeStruct(share, f32),
        ),
        in_specs=[smem] + [vmem] * 7,
        out_specs=(hbm,) * 4 + (vmem,),
        scratch_shapes=[
            held, held,
            pltpu.VMEM(window, bf16),
            pltpu.VMEM((1, 6 * HALF), f32),
            pltpu.VMEM((1, ch), f32),
            *half_scratch(tokens, ch),
            pltpu.SemaphoreType.DMA((slots,)),
            pltpu.SemaphoreType.DMA((kept,)),
            pltpu.SemaphoreType.DMA((1,)),
        ],
        compiler_params=pltpu.CompilerParams(vmem_limit_bytes=VMEM_LIMIT),
        cost_estimate=half_cost(tokens, patches, ch),
        name="second_half",
    )(plan, x, inv, nrm, ub, added, dn, oth)


def finish_kernel(
    plan_ref, parts_ref, back_c_ref, back_d_ref, grad_in_ref, grad_ref, total_ref, sems
):
    back = [back_c_ref.at[0], back_d_ref.at[0], back_d_ref.at[1]]
    copies = []
    for d in range(MOVES):
        s = plan_ref[LEAVES + d + 1]
        cp = pltpu.make_async_copy(back[d], grad_ref.at[jnp.maximum(s, 0)], sems.at[d])
        copies.append((s >= 0, cp))
    for moved, cp in copies:
        @pl.when(moved)
        def _(cp=cp):
            cp.start()

    n = parts_ref.shape[0]
    halves = []
    for h in range(2):
        total = parts_ref[1 - h].astype(f32)
        for z in range(1, n // 2):
            total = total + parts_ref[2 * z + 1 - h].astype(f32)
        halves.append(share_block(total))
    total_ref[...] = jnp.concatenate(halves, axis=1)
    for moved, cp in copies:
        @pl.when(moved)
        def _(cp=cp):
            cp.wait()


def finish(plan, parts, back_c, back_d, grad, rows):
    smem = pl.BlockSpec(memory_space=pltpu.SMEM)
    vmem = pl.BlockSpec(memory_space=pltpu.VMEM)
    hbm = pl.BlockSpec(memory_space=pl.ANY)
    return pl.pallas_call(
        finish_kernel,
        out_shape=(
            jax.ShapeDtypeStruct(grad.shape, bf16),
            jax.ShapeDtypeStruct((rows, 2 * HALF), f32),
        ),
        in_specs=[smem, vmem, vmem, vmem, hbm],
        out_specs=(hbm, vmem),
        scratch_shapes=[pltpu.SemaphoreType.DMA((MOVES,))],
        input_output_aliases={4: 0},
        compiler_params=pltpu.CompilerParams(vmem_limit_bytes=VMEM_LIMIT),
        name="finish",
    )(plan, parts, back_c, back_d, grad)


def shards(
    activations, cotangent, window_len, move_dest, move_slot, w_qkv, b_qkv, norm_gain, w_out
):
    n_shard = lax.axis_size("shard")
    rows = w_qkv.shape[0]
    tables = [t.transpose(2, 1, 0) for t in (window_len, move_dest, move_slot)]
    blob = pack(w_qkv, b_qkv[None], norm_gain[None], w_out.T, n_shard)
    own = lax.all_to_all(blob, "shard", 0, 0)
    par_a, par_b, plan = make_plan(tables, activations, blob)
    arr_a = permute_dp(par_a, 2)
    arr_b = permute_dp(jnp.stack([par_b, arr_a[1]]), 1)
    x, inv, ub = arrange(plan, activations, arr_a, arr_b, cotangent)
    own, x, inv, ub = lax.optimization_barrier((own, x, inv, ub))
    oth = swap_cores(own)
    nrm, added, dn, gt_out = first_half(plan, x, inv, ub, own)
    gt_in = swap_cores(gt_out)
    out, grad, ret_c, ret_d, gt = second_half(
        plan, x, inv, nrm, ub, added, dn, oth, activations.shape[0]
    )
    back_c = permute_dp(ret_c, -1)
    share = (gt + gt_in.astype(f32)).astype(bf16)
    chunks = lax.all_to_all(share, "shard", 0, 0)
    summed = jnp.sum(chunks.astype(f32), axis=0).astype(bf16)
    back_d = permute_dp(jnp.stack([ret_d, back_c[1]]), -2)
    parts = lax.all_gather(summed, "dp", axis=0)
    grad_input, total = finish(plan, parts, back_c, back_d, grad, rows)
    return (out, grad_input, total.T)


def solution(mesh):
    return jax.shard_map(
        shards,
        mesh=mesh,
        in_specs=(
            P(("dp", "shard"), None, None),
            P(("dp", "shard"), None, None),
            P(None, "shard", None),
            P(None, "shard", None),
            P(None, "shard", None),
            P("shard", None),
            P("shard"),
            P("shard"),
            P(None, "shard"),
        ),
        out_specs=(
            P(("dp", "shard"), None, None),
            P(("dp", "shard"), None, None),
            P(None, "shard"),
        ),
        check_vma=False,
    )
```

```python
import functools

import jax
import jax.numpy as jnp
from jax import lax
from jax.experimental import pallas as pl
from jax.experimental.pallas import tpu as pltpu
from jax.sharding import PartitionSpec as P

HEADS = 8
MOVES = 3
EPS = 1e-06
HALF = 320
PADH = 384
LANES = 128
CODES, LENS, STAYS, LEAVES, PLAN = 0, 16, 32, 48, 64
VMEM_LIMIT = 24 * 1024 * 1024
PACK_VMEM_LIMIT = 60 * 1024 * 1024

f32 = jnp.float32
bf16 = jnp.bfloat16


def permute_dp(array, by):
    n = lax.axis_size("dp")
    return lax.ppermute(array, "dp", [(i, (i + by) % n) for i in range(n)])


def swap_cores(array):
    n = lax.axis_size("dp")
    return lax.ppermute(array, "dp", [(i, i ^ 1) for i in range(n)])


def dot(a, b, ca, cb):
    return lax.dot_general(a, b, (((ca,), (cb,)), ((), ())), preferred_element_type=f32)


def tiles_of(groups):
    full = [g[:, t * LANES : (t + 1) * LANES] for g in groups for t in range(2)]
    half = [g[:, 2 * LANES : HALF] for g in groups]
    return full + [
        jnp.concatenate(half[0:2], axis=1),
        jnp.concatenate(half[2:4], axis=1),
    ]


def groups_of(tiles, rows):
    at = [tiles[t * rows : (t + 1) * rows] for t in range(10)]
    pad = jnp.zeros((rows, LANES // 2), f32)
    groups = []
    for g in range(4):
        both = at[8 + g // 2]
        half = both[:, (g % 2) * (LANES // 2) : (g % 2 + 1) * (LANES // 2)]
        groups.append(jnp.concatenate([at[2 * g], at[2 * g + 1], half, pad], axis=1))
    return groups


def share_tiles(x):
    low = x[0:24, 2 * LANES : HALF]
    high = jnp.concatenate([x[24:40, 2 * LANES : HALF], jnp.zeros((8, LANES // 2), f32)], axis=0)
    return jnp.concatenate(
        [x[:, 0:LANES], x[:, LANES : 2 * LANES], jnp.concatenate([low, high], axis=1)], axis=0
    )


def share_block(t):
    half = jnp.concatenate([t[80:104, 0 : LANES // 2], t[80:96, LANES // 2 :]], axis=0)
    return jnp.concatenate([t[0:40], t[40:80], half], axis=1)


SHARE = (104, LANES)


def pack_kernel(wqkv_ref, bias_ref, gain_ref, wout_ref, blob_ref, stage, sems):
    inner = wout_ref.shape[1]
    core = lax.rem(lax.axis_index("dp"), 2)
    tail = [
        jnp.pad(r[...].astype(f32), ((0, 0), (0, LANES - r.shape[1])))
        for r in (bias_ref, gain_ref)
    ] + [jnp.zeros((6, LANES), f32)]
    for c in range(2):
        @pl.when(core == c)
        def _(c=c):
            groups = [
                wqkv_ref[:, g * inner + c * HALF : g * inner + (c + 1) * HALF].astype(f32)
                for g in range(3)
            ] + [wout_ref[:, c * HALF : (c + 1) * HALF].astype(f32)]
            stage[...] = jnp.concatenate(tiles_of(groups) + tail, axis=0).astype(bf16)

    copies = [
        pltpu.make_async_copy(stage, blob_ref.at[s], sems.at[s]) for s in range(blob_ref.shape[0])
    ]
    for cp in copies:
        cp.start()
    for cp in copies:
        cp.wait()


def pack(wqkv, bias, gain, wout_t, n_shard):
    block_rows = 10 * wqkv.shape[0] + 8
    vmem = pl.BlockSpec(memory_space=pltpu.VMEM)
    hbm = pl.BlockSpec(memory_space=pl.ANY)
    return pl.pallas_call(
        pack_kernel,
        out_shape=jax.ShapeDtypeStruct((n_shard, block_rows, LANES), bf16),
        in_specs=[vmem] * 4,
        out_specs=hbm,
        scratch_shapes=[
            pltpu.VMEM((block_rows, LANES), bf16),
            pltpu.SemaphoreType.DMA((n_shard,)),
        ],
        compiler_params=pltpu.CompilerParams(vmem_limit_bytes=PACK_VMEM_LIMIT),
        name="pack_weights",
    )(wqkv, bias, gain, wout_t)


def plan_kernel(
    len_ref, dest_ref, slot_ref, act_ref, blob_ref, par_a_ref, par_b_ref, plan_ref, sems
):
    slots, _, n_dp = len_ref.shape
    me = lax.axis_index("dp")
    for i in range(plan_ref.shape[0]):
        plan_ref[i] = 0 if LENS <= i < STAYS else -1
    for s in range(slots):
        live = len_ref[s, 0, me] > 0
        dest = dest_ref[s, 0, me]

        @pl.when(live & (dest == me))
        def _(s=s):
            b = slot_ref[s, 0, me]
            plan_ref[CODES + b] = s
            plan_ref[LENS + b] = len_ref[s, 0, me]
            plan_ref[STAYS + s] = b

        for d in range(1, MOVES + 1):
            @pl.when(live & (dest == lax.rem(me + d, n_dp)))
            def _(d=d, s=s):
                plan_ref[LEAVES + d] = s

    leaving = [
        pltpu.make_async_copy(
            act_ref.at[jnp.maximum(plan_ref[LEAVES + d], 0)], to, sems.at[d - 1]
        )
        for d, to in ((1, par_b_ref), (2, par_a_ref.at[0]), (3, par_a_ref.at[1]))
    ]
    for cp in leaving:
        cp.start()
    for d in range(1, MOVES + 1):
        row = lax.rem(me - d + n_dp, n_dp)
        for s in range(slots):
            @pl.when((len_ref[s, 0, row] > 0) & (dest_ref[s, 0, row] == me))
            def _(d=d, s=s, row=row):
                b = slot_ref[s, 0, row]
                plan_ref[CODES + b] = slots + d - 1
                plan_ref[LENS + b] = len_ref[s, 0, row]

    for cp in leaving:
        cp.wait()


def make_plan(tables, act, blob):
    window = act.shape[1:]
    smem = pl.BlockSpec(memory_space=pltpu.SMEM)
    vmem = pl.BlockSpec(memory_space=pltpu.VMEM)
    hbm = pl.BlockSpec(memory_space=pl.ANY)
    return pl.pallas_call(
        plan_kernel,
        out_shape=(
            jax.ShapeDtypeStruct((2,) + window, bf16),
            jax.ShapeDtypeStruct(window, bf16),
            jax.ShapeDtypeStruct((PLAN,), jnp.int32),
        ),
        in_specs=[smem, smem, smem, hbm, hbm],
        out_specs=(vmem, vmem, smem),
        scratch_shapes=[pltpu.SemaphoreType.DMA((MOVES,))],
        compiler_params=pltpu.CompilerParams(vmem_limit_bytes=PACK_VMEM_LIMIT),
        cost_estimate=pl.CostEstimate(flops=0, bytes_accessed=4 * 1024 * 1024, transcendentals=0),
        name="make_plan",
    )(*tables, act, blob)


def arrange_kernel(
    plan_ref, act_ref, arr_a_ref, arr_b_ref, cot_ref, x_ref, inv_ref, ub_ref, cotb, win_sems, sem
):
    slots = act_ref.shape[0]
    kept, patches, ch = x_ref.shape
    cot_copy = pltpu.make_async_copy(cot_ref, cotb, sem.at[0])
    cot_copy.start()
    code = [plan_ref[CODES + b] for b in range(kept)]
    arrived = [arr_b_ref.at[0], arr_a_ref.at[0], arr_b_ref.at[1]]
    for b in range(kept):
        @pl.when((code[b] >= 0) & (code[b] < slots))
        def _(b=b):
            pltpu.make_async_copy(act_ref.at[code[b]], x_ref.at[b], win_sems.at[b]).start()

        for d in range(MOVES):
            @pl.when(code[b] == slots + d)
            def _(b=b, d=d):
                pltpu.make_async_copy(arrived[d], x_ref.at[b], win_sems.at[b]).start()

        @pl.when(code[b] < 0)
        def _(b=b):
            x_ref[b] = jnp.zeros((patches, ch), bf16)

    cot_copy.wait()
    position = lax.broadcasted_iota(jnp.int32, (patches, 1), 0)
    for b in range(kept):
        live = position < plan_ref[LENS + b]
        ub_ref[b * patches : (b + 1) * patches, :] = jnp.where(
            live, cotb[b].astype(f32), 0.0
        ).astype(bf16)
    for b in range(kept):
        @pl.when(code[b] >= 0)
        def _(b=b):
            pltpu.make_async_copy(act_ref.at[0], x_ref.at[b], win_sems.at[b]).wait()

        x = x_ref[b].astype(f32)
        inv = lax.rsqrt(jnp.mean(x * x, axis=-1, keepdims=True) + EPS)
        inv_ref[b * patches : (b + 1) * patches, :] = jnp.broadcast_to(inv, (patches, LANES))


def arrange(plan, act, arr_a, arr_b, cot):
    kept, patches, ch = cot.shape
    smem = pl.BlockSpec(memory_space=pltpu.SMEM)
    vmem = pl.BlockSpec(memory_space=pltpu.VMEM)
    hbm = pl.BlockSpec(memory_space=pl.ANY)
    return pl.pallas_call(
        arrange_kernel,
        out_shape=(
            jax.ShapeDtypeStruct(cot.shape, bf16),
            jax.ShapeDtypeStruct((kept * patches, LANES), f32),
            jax.ShapeDtypeStruct((kept * patches, ch), bf16),
        ),
        in_specs=[smem] + [hbm] * 4,
        out_specs=(vmem,) * 3,
        scratch_shapes=[
            pltpu.VMEM(cot.shape, bf16),
            pltpu.SemaphoreType.DMA((kept,)),
            pltpu.SemaphoreType.DMA((1,)),
        ],
        compiler_params=pltpu.CompilerParams(vmem_limit_bytes=VMEM_LIMIT // 3),
        cost_estimate=pl.CostEstimate(flops=0, bytes_accessed=8 * 1024 * 1024, transcendentals=0),
        name="arrange_windows",
    )(plan, act, arr_a, arr_b, cot)


def unpack_weights(g, wqkv, wo, bias_row, gain_row):
    n_shard = g.shape[0]
    rows = g.shape[1] // 10
    for s in range(n_shard):
        tail = g[s].astype(f32)[10 * rows :]
        bias_row[0:1, 3 * rows * s : 3 * rows * (s + 1)] = tail[0:1, 0 : 3 * rows]
        gain_row[0:1, rows * s : rows * (s + 1)] = tail[1:2, 0:rows]
    for t in range(n_shard // 2):
        pair = [groups_of(g[2 * t + i].astype(f32), rows) for i in range(2)]
        at = pl.ds(2 * rows * t, 2 * rows)
        for k in range(4):
            piece = jnp.concatenate([pair[0][k], pair[1][k]], axis=0).astype(bf16)
            if k < 3:
                wqkv[at, k * PADH : (k + 1) * PADH] = piece
            else:
                wo[at, :] = piece


def bias_of(bias_row, low_half):
    parts = []
    for k in range(3):
        low = bias_row[0:1, 2 * k * HALF : (2 * k + 1) * HALF]
        high = bias_row[0:1, (2 * k + 1) * HALF : (2 * k + 2) * HALF]
        parts += [jnp.where(low_half, low, high), jnp.zeros((1, PADH - HALF), f32)]
    return jnp.concatenate(parts, axis=1)


def attention(lens, patches, qkv, da, att, dproj):
    head = HALF // 4
    scale = head ** (-0.5)
    starts = (0, LANES)
    lane = lax.broadcasted_iota(jnp.int32, (patches, 2 * LANES), 1)
    masks = []
    for i in range(4):
        low = i * head - starts[i // 2]
        masks.append(((lane >= low) & (lane < low + head)).astype(f32).astype(bf16))
    key_pos = lax.broadcasted_iota(jnp.int32, (patches, 2 * patches), 0)

    def by_head(m, g):
        return jnp.concatenate([m * masks[2 * g], m * masks[2 * g + 1]], axis=0)

    def joined(a, b):
        return jnp.concatenate(
            [a[:, :LANES], a[:, LANES:] + b[:, :LANES], b[:, LANES:]], axis=1
        ).astype(bf16)

    def stacked(m):
        return jnp.concatenate([m[:, :patches], m[:, patches:]], axis=0)

    def scored(w, g):
        at = pl.ds(w * patches, patches)
        low = starts[g]
        q, k, v = [qkv[at, i * PADH + low : i * PADH + low + 2 * LANES] for i in range(3)]
        q_heads = by_head(q, g)
        d_heads = by_head(da[at, low : low + 2 * LANES], g)
        return q_heads, d_heads, k, v, dot(k, q_heads, 1, 1), dot(v, d_heads, 1, 1)

    def softmaxed(w, g, q_heads, d_heads, k, v, scores, d_probs):
        allowed = key_pos < jnp.maximum(lens[w], 1)
        weights = jnp.where(allowed, jnp.exp(scores * scale), 0.0)
        probs = weights * (1.0 / jnp.sum(weights, axis=0, keepdims=True))
        d_probs = d_probs.astype(bf16).astype(f32)
        mean = jnp.sum(d_probs * probs, axis=0, keepdims=True)
        d_scores = (probs * (d_probs - mean) * scale).astype(bf16)
        return q_heads, d_heads, k, v, probs.astype(bf16), d_scores

    def combined(w, g, q_heads, d_heads, k, v, probs, d_scores):
        return (
            dot(stacked(probs), by_head(v, g), 0, 0),
            dot(stacked(d_scores), by_head(k, g), 0, 0),
            dot(d_scores, q_heads, 1, 0),
            dot(probs, d_heads, 1, 0),
        )

    todo = [(w, g) for w in range(len(lens)) for g in range(2)]
    step = 14
    for first in range(0, len(todo), step):
        some = todo[first : first + step]
        state = [scored(*p) for p in some]
        state = [softmaxed(*p, *c) for p, c in zip(some, state)]
        state = [combined(*p, *c) for p, c in zip(some, state)]
        for i in range(0, len(some), 2):
            at = pl.ds(some[i][0] * patches, patches)
            o, dq, dk, dv = [joined(x, y) for x, y in zip(state[i], state[i + 1])]
            att[at, :] = o
            dproj[at, 0:PADH] = dq
            dproj[at, PADH : 2 * PADH] = dk
            dproj[at, 2 * PADH :] = dv


def first_half_kernel(
    plan_ref, xb, inv_ref, ub, g_ref, nrm, added, dn, gt,
    bias_row, gain_row, wqkv, wo, qkv, da, att, dproj,
):
    kept, patches, ch = xb.shape
    n_shard = g_ref.shape[0]
    rows = g_ref.shape[1] // 10
    core = lax.rem(lax.axis_index("dp"), 2)
    lens = [plan_ref[LENS + b] for b in range(kept)]
    unpack_weights(g_ref, wqkv, wo, bias_row, gain_row)
    bias = bias_of(bias_row, core == 0)
    gain = gain_row[...]
    for b in range(kept):
        at = slice(b * patches, (b + 1) * patches)
        inv = jnp.concatenate([inv_ref[at, :]] * (ch // LANES), axis=1)
        nrm[at, :] = (xb[b].astype(f32) * inv * gain).astype(bf16)
    qkv[...] = (dot(nrm[...], wqkv[...], 1, 0) + bias).astype(bf16)
    da[...] = dot(ub[...], wo[...], 1, 0).astype(bf16)
    attention(lens, patches, qkv, da, att, dproj)
    whole = dot(ub[...], att[...], 0, 0)
    for s in range(n_shard):
        gt[s] = share_tiles(whole[s * rows : (s + 1) * rows]).astype(bf16)
    added[...] = dot(att[...], wo[...], 1, 1)
    dn[...] = dot(dproj[...], wqkv[...], 1, 1)


def second_half_kernel(
    plan_ref, xb, inv_ref, nrm, ub, added, dn, g_ref,
    out_ref, grad_ref, ret_1_ref, ret_2_ref, ret_3_ref, gt,
    outb, gbuf, zeros, bias_row, gain_row, wqkv, wo, qkv, da, att, dproj,
    zero_sems, win_sems, out_sem,
):
    slots = grad_ref.shape[0]
    kept, patches, ch = xb.shape
    n_shard = g_ref.shape[0]
    rows = g_ref.shape[1] // 10
    core = lax.rem(lax.axis_index("dp"), 2)
    zeros[...] = jnp.zeros(zeros.shape, bf16)
    code = [plan_ref[CODES + b] for b in range(kept)]
    lens = [plan_ref[LENS + b] for b in range(kept)]

    def zero_copy(s):
        return pltpu.make_async_copy(zeros, grad_ref.at[s], zero_sems.at[s])

    for s in range(slots):
        @pl.when(plan_ref[STAYS + s] < 0)
        def _(s=s):
            zero_copy(s).start()

    returned = [ret_1_ref, ret_2_ref, ret_3_ref]

    def ready(b):
        @pl.when((code[b] >= 0) & (code[b] < slots))
        def _():
            pltpu.make_async_copy(gbuf.at[b], grad_ref.at[code[b]], win_sems.at[b]).start()

        for d in range(MOVES):
            @pl.when(code[b] == slots + d)
            def _(d=d):
                pltpu.make_async_copy(gbuf.at[b], returned[d], win_sems.at[b]).start()

    unpack_weights(g_ref, wqkv, wo, bias_row, gain_row)
    bias = bias_of(bias_row, core == 1)
    gain = gain_row[...]
    qkv[...] = (dot(nrm[...], wqkv[...], 1, 0) + bias).astype(bf16)
    da[...] = dot(ub[...], wo[...], 1, 0).astype(bf16)
    attention(lens, patches, qkv, da, att, dproj)
    whole = dot(ub[...], att[...], 0, 0)
    for s in range(n_shard):
        gt[s] = share_tiles(whole[s * rows : (s + 1) * rows])
    position = lax.broadcasted_iota(jnp.int32, (patches, 1), 0)
    total = added[...] + dot(att[...], wo[...], 1, 1)
    for b in range(kept):
        at = slice(b * patches, (b + 1) * patches)
        outb[b] = jnp.where(position < lens[b], xb[b].astype(f32) + total[at], 0.0).astype(bf16)
    out_copy = pltpu.make_async_copy(outb, out_ref, out_sem.at[0])
    out_copy.start()
    d_nrm = dn[...] + dot(dproj[...], wqkv[...], 1, 1)
    for b in range(kept):
        at = slice(b * patches, (b + 1) * patches)
        x = xb[b].astype(f32)
        inv = jnp.concatenate([inv_ref[at, :]] * (ch // LANES), axis=1)
        t = d_nrm[at].astype(bf16).astype(f32) * gain
        along = jnp.mean(t * x, axis=-1, keepdims=True)
        dx = t * inv - x * (inv * inv * inv * along)
        gbuf[b] = (ub[at, :].astype(f32) + dx).astype(bf16)
        ready(b)

    for b in range(kept):
        @pl.when(code[b] >= 0)
        def _(b=b):
            pltpu.make_async_copy(gbuf.at[b], grad_ref.at[0], win_sems.at[b]).wait()
    for s in range(slots):
        @pl.when(plan_ref[STAYS + s] < 0)
        def _(s=s):
            zero_copy(s).wait()
    out_copy.wait()


def half_cost(tokens, patches, ch):
    work = 2 * tokens * HALF * (9 * ch + 6 * patches)
    return pl.CostEstimate(flops=work, bytes_accessed=8 * 1024 * 1024, transcendentals=4 * tokens * patches)


def half_scratch(tokens, ch):
    return [
        pltpu.VMEM((ch, 3 * PADH), bf16),
        pltpu.VMEM((ch, PADH), bf16),
        pltpu.VMEM((tokens, 3 * PADH), bf16),
        pltpu.VMEM((tokens, PADH), bf16),
        pltpu.VMEM((tokens, PADH), bf16),
        pltpu.VMEM((tokens, 3 * PADH), bf16),
    ]


def first_half(plan, x, inv, ub, own):
    kept, patches, ch = x.shape
    tokens = kept * patches
    share = (own.shape[0],) + SHARE
    smem = pl.BlockSpec(memory_space=pltpu.SMEM)
    vmem = pl.BlockSpec(memory_space=pltpu.VMEM)
    return pl.pallas_call(
        first_half_kernel,
        out_shape=(
            jax.ShapeDtypeStruct((tokens, ch), bf16),
            jax.ShapeDtypeStruct((tokens, ch), f32),
            jax.ShapeDtypeStruct((tokens, ch), f32),
            jax.ShapeDtypeStruct(share, bf16),
        ),
        in_specs=[smem, vmem, vmem, vmem, vmem],
        out_specs=(vmem,) * 4,
        scratch_shapes=[
            pltpu.VMEM((1, 6 * HALF), f32),
            pltpu.VMEM((1, ch), f32),
            *half_scratch(tokens, ch),
        ],
        compiler_params=pltpu.CompilerParams(vmem_limit_bytes=VMEM_LIMIT),
        cost_estimate=half_cost(tokens, patches, ch),
        name="first_half",
    )(plan, x, inv, ub, own)


def second_half(plan, x, inv, nrm, ub, added, dn, oth, slots):
    kept, patches, ch = x.shape
    tokens = kept * patches
    share = (oth.shape[0],) + SHARE
    window = (patches, ch)
    smem = pl.BlockSpec(memory_space=pltpu.SMEM)
    vmem = pl.BlockSpec(memory_space=pltpu.VMEM)
    hbm = pl.BlockSpec(memory_space=pl.ANY)
    held = pltpu.VMEM(x.shape, bf16)
    return pl.pallas_call(
        second_half_kernel,
        out_shape=(
            jax.ShapeDtypeStruct(x.shape, bf16),
            jax.ShapeDtypeStruct((slots,) + window, bf16),
            jax.ShapeDtypeStruct(window, bf16),
            jax.ShapeDtypeStruct(window, bf16),
            jax.ShapeDtypeStruct(window, bf16),
            jax.ShapeDtypeStruct(share, f32),
        ),
        in_specs=[smem] + [vmem] * 7,
        out_specs=(hbm,) * 5 + (vmem,),
        scratch_shapes=[
            held, held,
            pltpu.VMEM(window, bf16),
            pltpu.VMEM((1, 6 * HALF), f32),
            pltpu.VMEM((1, ch), f32),
            *half_scratch(tokens, ch),
            pltpu.SemaphoreType.DMA((slots,)),
            pltpu.SemaphoreType.DMA((kept,)),
            pltpu.SemaphoreType.DMA((1,)),
        ],
        compiler_params=pltpu.CompilerParams(vmem_limit_bytes=VMEM_LIMIT),
        cost_estimate=half_cost(tokens, patches, ch),
        name="second_half",
    )(plan, x, inv, nrm, ub, added, dn, oth)


def finish_kernel(
    plan_ref, parts_ref, back_1_ref, back_2_ref, back_3_ref, grad_in_ref, grad_ref, total_ref, sems
):
    back = [back_1_ref, back_2_ref, back_3_ref]
    copies = []
    for d in range(MOVES):
        s = plan_ref[LEAVES + d + 1]
        cp = pltpu.make_async_copy(back[d], grad_ref.at[jnp.maximum(s, 0)], sems.at[d])
        copies.append((s >= 0, cp))
    for moved, cp in copies:
        @pl.when(moved)
        def _(cp=cp):
            cp.start()

    n = parts_ref.shape[0]
    halves = []
    for h in range(2):
        total = parts_ref[1 - h].astype(f32)
        for z in range(1, n // 2):
            total = total + parts_ref[2 * z + 1 - h].astype(f32)
        halves.append(share_block(total))
    total_ref[...] = jnp.concatenate(halves, axis=1)
    for moved, cp in copies:
        @pl.when(moved)
        def _(cp=cp):
            cp.wait()


def finish(plan, parts, back, grad, rows):
    smem = pl.BlockSpec(memory_space=pltpu.SMEM)
    vmem = pl.BlockSpec(memory_space=pltpu.VMEM)
    hbm = pl.BlockSpec(memory_space=pl.ANY)
    return pl.pallas_call(
        finish_kernel,
        out_shape=(
            jax.ShapeDtypeStruct(grad.shape, bf16),
            jax.ShapeDtypeStruct((rows, 2 * HALF), f32),
        ),
        in_specs=[smem, vmem, vmem, vmem, vmem, hbm],
        out_specs=(hbm, vmem),
        scratch_shapes=[pltpu.SemaphoreType.DMA((MOVES,))],
        input_output_aliases={5: 0},
        compiler_params=pltpu.CompilerParams(vmem_limit_bytes=VMEM_LIMIT),
        name="finish",
    )(plan, parts, *back, grad)


def shards(
    activations, cotangent, window_len, move_dest, move_slot, w_qkv, b_qkv, norm_gain, w_out
):
    n_shard = lax.axis_size("shard")
    rows = w_qkv.shape[0]
    tables = [t.transpose(2, 1, 0) for t in (window_len, move_dest, move_slot)]
    blob = pack(w_qkv, b_qkv[None], norm_gain[None], w_out.T, n_shard)
    own = lax.all_to_all(blob, "shard", 0, 0)
    par_a, par_b, plan = make_plan(tables, activations, blob)
    arr_a = permute_dp(par_a, 2)
    arr_b = permute_dp(jnp.stack([par_b, arr_a[1]]), 1)
    x, inv, ub = arrange(plan, activations, arr_a, arr_b, cotangent)
    own, x, inv, ub = lax.optimization_barrier((own, x, inv, ub))
    oth = swap_cores(own)
    nrm, added, dn, gt_out = first_half(plan, x, inv, ub, own)
    gt_in = swap_cores(gt_out)
    out, grad, *returned, gt = second_half(
        plan, x, inv, nrm, ub, added, dn, oth, activations.shape[0]
    )
    back = [permute_dp(r, -d) for d, r in enumerate(returned, 1)]
    share = (gt + gt_in.astype(f32)).astype(bf16)
    chunks = lax.all_to_all(share, "shard", 0, 0)
    summed = jnp.sum(chunks.astype(f32), axis=0).astype(bf16)
    parts = lax.all_gather(summed, "dp", axis=0)
    grad_input, total = finish(plan, parts, back, grad, rows)
    return (out, grad_input, total.T)


def solution(mesh):
    return jax.shard_map(
        shards,
        mesh=mesh,
        in_specs=(
            P(("dp", "shard"), None, None),
            P(("dp", "shard"), None, None),
            P(None, "shard", None),
            P(None, "shard", None),
            P(None, "shard", None),
            P("shard", None),
            P("shard"),
            P("shard"),
            P(None, "shard"),
        ),
        out_specs=(
            P(("dp", "shard"), None, None),
            P(("dp", "shard"), None, None),
            P(None, "shard"),
        ),
        check_vma=False,
    )
```
